256 devices in a mesh: store: 32 (over x_lo, z, core), tp: 8 (over y, x_hi).
Axes of the slice: x: 4 (x_hi: 2, x_lo: 2; x = x_hi * 2 + x_lo), y: 4, z: 8, core: 2. Of those that a mesh axis runs over, the one named last changes fastest.
Arguments:
- queries: bfloat16 [4096, 8192], P('store', 'tp'), may hold values from -80 to 80
- kv_new: bfloat16 [4096, 2048], P('store', 'tp'), may hold values from -4 to 4
- page_pool: bfloat16 [1024, 256, 2048], P('store', None, 'tp'), may hold values from -6 to 6
- hit_owner: int32 [32, 36], P('store'), may hold values from 0 to 31, as said below
- hit_page: int32 [32, 36], P('store'), may hold values from 0 to 31
- prefix_blocks: int32 [32], P('store'), may hold values from 20 to 28, as said below
- suffix_len: int32 [32], P('store'), may hold values from 32 to 128, as said below
- out_weight: bfloat16 [8192, 8192], P('tp', 'store'), may hold values from -0.0625 to 0.0625
- mamba_x: bfloat16 [4096, 16384], P('store', 'tp'), may hold values from -6 to 6
- mamba_z: bfloat16 [4096, 16384], P('store', 'tp'), may hold values from -6 to 6
- mamba_b: bfloat16 [4096, 2048], P('store', 'tp'), may hold values from -6 to 6
- mamba_c: bfloat16 [4096, 2048], P('store', 'tp'), may hold values from -0.59765625 to 0.59765625
- mamba_dt: float32 [4096, 256], P('store', 'tp'), may hold values from 0 to 0.3
- a_log: float32 [256], P('tp'), may hold values from 0 to 1.386
- d_skip: float32 [256], P('tp'), may hold values from 0.5 to 1.5
- norm_gain: float32 [16384], P('tp'), may hold values from 0.5 to 1.5
Outputs:
- attn_proj: bfloat16 [4096, 8192], P('store', 'tp')
- mamba_out: bfloat16 [4096, 16384], P('store', 'tp')
The draws below stay inside these ranges and needn't reach their ends.
Inputs may be any that keep to these rules, and one draw needn't show every extreme that they name: `hit_owner`: each request names at most 2 hits at one owner, and in every request some owner is named exactly 2 times. `prefix_blocks`: some request uses all 28 prefix pages. `suffix_len`: some request has 128 live tokens.
All inputs are finite; a program needn't handle non-finite values.
Results may differ from the reference program's by a relative error of at most 0.02.
Values may be sent and summed in bfloat16 or wider, within the bound.
No kernel may reach another device: no remote copies, remote signals or barrier semaphores. Data moves between devices by JAX's collectives and lax.ppermute only.
A program may use at most 128 MiB of HBM per device.

```python
import jax
import jax.numpy as jnp
from jax import lax

D = 8192
QH = 64
KVH = 8
HD = 128
MH = 256
MP = 64
NS = 256
NG = 8
PAGE = 256
SP = 8
CAP = 2
MBLOCK = 128
TAIL_WORDS = 128
PMAX = 28
PAGES_DEV = 32
HITS = 36
TOKENS = 4096
N_STORE = 32


def shared_keys(key):
    payload_lines = jax.random.normal(key, (TOKENS, KVH * 2 * HD), jnp.float32)
    return jnp.clip(payload_lines, -4.0, 4.0)


def draw_kv_new(key, part):
    payload_lines = shared_keys(key)
    return payload_lines.astype(jnp.bfloat16)


def draw_queries(key, part):
    key = jax.random.fold_in(key, 43)
    payload_lines = jax.random.normal(key, (TOKENS, QH * HD), jnp.float32)
    return payload_lines.astype(jnp.bfloat16)


def draw_mamba_dt(key, part):
    key = jax.random.fold_in(key, 11)
    attention_lane_seed, approximate_seed, query_job_seed, spike_seed_handle = jax.random.split(key, 4)
    overall_tally = TOKENS // TAIL_WORDS
    lowest, highest = (0.002, 0.04)
    starting_magnitude = jnp.exp(jax.random.uniform(attention_lane_seed, (1, 1, MH), jnp.float32, jnp.log(lowest), jnp.log(highest)))
    approximate_guess = jax.random.uniform(approximate_seed, (overall_tally, TAIL_WORDS, MH), jnp.float32, 0.5, 1.5)
    query_job_multiplier = jnp.exp(jax.random.uniform(query_job_seed, (overall_tally, 1, 1), jnp.float32, jnp.log(0.5), jnp.log(2.0)))
    spike_line_sequence = jax.random.randint(spike_seed_handle, (overall_tally, 3), 0, TAIL_WORDS)
    spike_batches = jnp.any(jnp.arange(TAIL_WORDS)[None, :, None] == spike_line_sequence[:, None, :], axis=-1).astype(jnp.float32)
    payload_lines = starting_magnitude * approximate_guess * query_job_multiplier + 0.15 * spike_batches[:, :, None]
    return payload_lines.reshape(TOKENS, MH)


def draw_hit_owner(key, part):
    key = jax.random.fold_in(key, 51)
    overall_tally = TOKENS // TAIL_WORDS
    slot_total = CAP * overall_tally
    low_live = max(2, PMAX * 5 // 7)
    request_keys = jax.random.split(key, overall_tally)

    def one_request(query_job_seed):
        shuffle_key, place_key = jax.random.split(query_job_seed)
        shuffled = jax.random.permutation(shuffle_key, slot_total)
        leader = shuffled[0]
        partner = leader // CAP * CAP + (leader % CAP + 1) % CAP
        partner_at = jnp.argmax(shuffled == partner)
        target = jax.random.randint(place_key, (), 1, low_live)
        displaced = shuffled[target]
        shuffled = shuffled.at[partner_at].set(displaced).at[target].set(partner)
        return (shuffled[:HITS] // CAP).astype(jnp.int32)
    return jax.vmap(one_request)(request_keys)


def draw_prefix_blocks(key, part):
    key = jax.random.fold_in(key, 61)
    first_key, second_key = jax.random.split(key)
    overall_tally = TOKENS // TAIL_WORDS
    drawn = jax.random.randint(first_key, (overall_tally,), max(2, PMAX * 5 // 7), PMAX + 1)
    chosen = jax.random.randint(second_key, (), 0, overall_tally)
    return jnp.where(jnp.arange(overall_tally) == chosen, PMAX, drawn).astype(jnp.int32)


def draw_suffix_len(key, part):
    key = jax.random.fold_in(key, 71)
    first_key, second_key = jax.random.split(key)
    overall_tally = TOKENS // TAIL_WORDS
    drawn = jax.random.randint(first_key, (overall_tally,), max(4, TAIL_WORDS // 4), TAIL_WORDS + 1)
    chosen = jax.random.randint(second_key, (), 0, overall_tally)
    return jnp.where(jnp.arange(overall_tally) == chosen, TAIL_WORDS, drawn).astype(jnp.int32)


def touch_ends(values, key, smallest, top_value):
    longest = values.shape.index(max(values.shape))
    spots = []
    for shift in (0, 1):
        where = [jax.random.randint(jax.random.fold_in(key, axis), (), 0, length) for axis, length in enumerate(values.shape)]
        where[longest] = (where[longest] + shift) % values.shape[longest]
        spots.append(tuple(where))
    return values.at[spots[0]].set(smallest).at[spots[1]].set(top_value)


def block_levels(key, extent, shards, smallest, largest):
    level, own = 1.0, jax.random.fold_in(key, 6)
    for axis_at, blocks in shards:
        draws = jnp.exp(jax.random.uniform(jax.random.fold_in(own, axis_at), (blocks,), jnp.float32, smallest / len(shards), largest / len(shards)))
        level = level * jnp.repeat(draws, extent[axis_at] // blocks).reshape([-1 if axis == axis_at else 1 for axis in range(len(extent))])
    return level


def gaussian(key, dims, width, reach, cuts=(), held_as=jnp.bfloat16):
    entries = width * jax.random.normal(key, dims, jnp.float32)
    if cuts:
        entries = entries * block_levels(key, dims, cuts, -0.22, 0.18)
    return jnp.clip(entries, -reach, reach).astype(held_as)


def setup_inputs(seed: int = 0) -> dict:
    seeds = jax.random.split(jax.random.key(seed), 17)
    return {
        "queries": draw_queries(jax.random.fold_in(seeds[16], 71), 0),
        "kv_new": draw_kv_new(jax.random.fold_in(seeds[16], 71), 0),
        "page_pool": gaussian(seeds[2], (N_STORE * PAGES_DEV, PAGE, KVH * 2 * HD), 1.0, 6.0, ((0, 32), (2, 8))),
        "hit_owner": draw_hit_owner(jax.random.fold_in(seeds[16], 71), 0),
        "hit_page": touch_ends(jax.random.randint(seeds[4], (N_STORE, HITS), 0, PAGES_DEV), jax.random.fold_in(seeds[4], 1), 0, PAGES_DEV - 1).astype(jnp.int32),
        "prefix_blocks": draw_prefix_blocks(jax.random.fold_in(seeds[16], 71), 0),
        "suffix_len": draw_suffix_len(jax.random.fold_in(seeds[16], 71), 0),
        "out_weight": gaussian(seeds[7], (QH * HD, D), (QH * HD) ** -0.5, 0.0625, ((0, 8), (1, 32))),
        "mamba_x": gaussian(seeds[8], (TOKENS, MH * MP), 1.0, 6.0, ((0, 32), (1, 8))),
        "mamba_z": gaussian(seeds[9], (TOKENS, MH * MP), 1.0, 6.0, ((0, 32), (1, 8))),
        "mamba_b": gaussian(seeds[10], (TOKENS, NG * NS), 1.0, 6.0, ((0, 32), (1, 8))),
        "mamba_c": gaussian(seeds[11], (TOKENS, NG * NS), 0.1, 0.59765625, ((0, 32), (1, 8))),
        "mamba_dt": draw_mamba_dt(jax.random.fold_in(seeds[16], 71), 0),
        "a_log": jnp.clip(1.386 * jax.random.uniform(seeds[13], (MH,), jnp.float32) ** block_levels(seeds[13], (MH,), ((0, 8),), -0.2, 0.2), 0.0, 1.386),
        "d_skip": jnp.clip(0.5 + 1.0 * jax.random.uniform(seeds[14], (MH,), jnp.float32) ** block_levels(seeds[14], (MH,), ((0, 8),), -0.2, 0.2), 0.5, 1.5),
        "norm_gain": jnp.clip(1.0 + 0.1 * jax.random.normal(seeds[15], (MH * MP,), jnp.float32), 0.5, 1.5),
    }


HIGHEST_PRECISION = lax.Precision.HIGHEST
MASKED = -1e+30

def ssd_block(ssm_state, x_block, b_block, c_block, dt_block, log_decay, d_skip):
    length = x_block.shape[0]
    head_count = x_block.shape[1]
    head_width = x_block.shape[2]
    groups = b_block.shape[1]
    per_group = head_count // groups
    running = jnp.cumsum(log_decay, axis=0)
    causal = jnp.arange(length)[:, None] >= jnp.arange(length)[None, :]
    spread = jnp.where(causal[None], running.T[:, :, None] - running.T[:, None, :], MASKED)
    decay_table = jnp.exp(spread).reshape(groups, per_group, length, length)
    inner_prod = jnp.einsum('tgn,sgn->gts', c_block, b_block, precision=HIGHEST_PRECISION)
    mixing = decay_table * inner_prod[:, None]
    scaled = (x_block * dt_block[:, :, None]).reshape(length, groups, per_group, head_width)
    within = jnp.einsum('gjts,sgjp->tgjp', mixing, scaled, precision=HIGHEST_PRECISION)
    carried = jnp.einsum('tgn,gjpn->tgjp', c_block, ssm_state.reshape(groups, per_group, head_width, -1), precision=HIGHEST_PRECISION)
    output = within.reshape(length, head_count, head_width) + jnp.exp(running)[:, :, None] * carried.reshape(length, head_count, head_width) + d_skip[None, :, None] * x_block
    to_end = jnp.exp(running[-1][None, :] - running)
    weighted = (x_block * (dt_block * to_end)[:, :, None]).reshape(length, groups, per_group, head_width)
    injected = jnp.einsum('sgjp,sgn->gjpn', weighted, b_block, precision=HIGHEST_PRECISION).reshape(ssm_state.shape)
    new_state = jnp.exp(running[-1])[:, None, None] * ssm_state + injected
    return (new_state, output)

def gated_norm(payload_lines, gate_rows, gain_vector, groups, valid_rows):
    row_count = payload_lines.shape[0]
    mixed = payload_lines.reshape(row_count, -1) * jax.nn.silu(gate_rows.astype(jnp.float32))
    grouped = mixed.reshape(row_count, groups, -1)
    mean_square = lax.optimization_barrier(jnp.mean(grouped * grouped, axis=-1, keepdims=True))
    normed = grouped * lax.rsqrt(mean_square + 1e-05) * gain_vector.reshape(groups, -1)[None]
    normed = jnp.where(valid_rows[:, None], normed.reshape(row_count, -1), 0.0)
    return normed.astype(jnp.bfloat16)

def reference(queries, kv_new, page_pool, hit_owner, hit_page, prefix_blocks, suffix_len, out_weight, mamba_x, mamba_z, mamba_b, mamba_c, mamba_dt, a_log, d_skip, norm_gain):
    group_size = QH // KVH
    position = jnp.arange(TAIL_WORDS)
    block_count = TAIL_WORDS // MBLOCK

    def attend(request):
        page_index = hit_owner[request] * PAGES_DEV + hit_page[request]
        prefix_keys = page_pool[page_index[:PMAX]].reshape(PMAX * PAGE, KVH, 2, HD)
        row_start = (request * TAIL_WORDS).astype(jnp.int32)
        recent = lax.dynamic_slice_in_dim(kv_new, row_start, TAIL_WORDS, 0).reshape(TAIL_WORDS, KVH, 2, HD)
        all_keys = jnp.concatenate([prefix_keys, recent], axis=0).astype(jnp.float32)
        query_rows = lax.dynamic_slice_in_dim(queries, row_start, TAIL_WORDS, 0).reshape(TAIL_WORDS, KVH, group_size, HD).astype(jnp.float32)
        scores = jnp.einsum('tkgd,skd->kgts', query_rows, all_keys[:, :, 0], precision=HIGHEST_PRECISION) * HD ** (-0.5)
        length = suffix_len[request]
        seen_prefix = jnp.arange(PMAX * PAGE) < prefix_blocks[request] * PAGE
        seen_recent = (position[None, :] <= position[:, None]) & (position[None, :] < length)
        visible = jnp.concatenate([jnp.broadcast_to(seen_prefix[None, :], (TAIL_WORDS, PMAX * PAGE)), seen_recent], axis=1)
        scores = jnp.where(visible, scores, MASKED)
        row_max = lax.optimization_barrier(jnp.max(scores, axis=-1, keepdims=True))
        exponent = jnp.exp(scores - row_max)
        rounded = lax.optimization_barrier(exponent.astype(jnp.bfloat16)).astype(jnp.float32)
        summed = jnp.einsum('kgts,skd->kgtd', rounded, all_keys[:, :, 1], precision=HIGHEST_PRECISION)
        result = summed / lax.optimization_barrier(jnp.sum(exponent, axis=-1))[..., None]
        result = result.transpose(2, 0, 1, 3).reshape(TAIL_WORDS, QH * HD)
        result = jnp.where((position < length)[:, None], result, 0.0)
        return result.astype(jnp.bfloat16)
    attn_out = lax.map(attend, jnp.arange(N_STORE, dtype=jnp.int32)).reshape(TOKENS, QH * HD)
    attn_proj = jnp.dot(attn_out, out_weight, preferred_element_type=jnp.float32).astype(jnp.bfloat16)

    def recurrent(request):
        page_index = hit_owner[request] * PAGES_DEV + hit_page[request]
        saved_pages = page_pool[page_index[PMAX:]].astype(jnp.float32)
        ssm_state = saved_pages.reshape(SP, PAGE, KVH, 2 * HD).transpose(2, 0, 1, 3).reshape(MH, MP, NS)
        row_start = (request * TAIL_WORDS).astype(jnp.int32)
        x_rows = lax.dynamic_slice_in_dim(mamba_x, row_start, TAIL_WORDS, 0).astype(jnp.float32).reshape(block_count, MBLOCK, MH, MP)
        z_rows = lax.dynamic_slice_in_dim(mamba_z, row_start, TAIL_WORDS, 0)
        b_rows = lax.dynamic_slice_in_dim(mamba_b, row_start, TAIL_WORDS, 0).astype(jnp.float32).reshape(block_count, MBLOCK, NG, NS)
        c_rows = lax.dynamic_slice_in_dim(mamba_c, row_start, TAIL_WORDS, 0).astype(jnp.float32).reshape(block_count, MBLOCK, NG, NS)
        dt_rows = lax.dynamic_slice_in_dim(mamba_dt, row_start, TAIL_WORDS, 0).reshape(block_count, MBLOCK, MH)
        log_decay = -jnp.exp(a_log)[None, None, :] * dt_rows

        def advance(ssm_carry, block_data):
            return ssd_block(ssm_carry, block_data[0], block_data[1], block_data[2], block_data[3], block_data[4], d_skip)
        last_state, outputs = lax.scan(advance, ssm_state, (x_rows, b_rows, c_rows, dt_rows, log_decay))
        return gated_norm(outputs.reshape(TAIL_WORDS, MH, MP), z_rows, norm_gain, NG, position < suffix_len[request])
    mamba_out = lax.map(recurrent, jnp.arange(N_STORE, dtype=jnp.int32)).reshape(TOKENS, MH * MP)
    return (attn_proj, mamba_out)
```

```python
import functools

import jax
import jax.numpy as jnp
from jax import lax
from jax.experimental import pallas as pl
from jax.experimental.pallas import tpu as pltpu
from jax.sharding import Mesh, PartitionSpec as P

HD = 128
HEADS = 8
NS = 256
PAGE = 256
SP = 8
CAP = 2
PMAX = 28
HITS = 36
POOL = 32
ROWS = 128
NZ = 8
NTP = 8
VISITS = 32
MASKED = -1e30
SCALE = HD ** (-0.5) * 1.4426950408889634
F32 = jnp.float32
BF16 = jnp.bfloat16
VMEM_LIMIT = 56 * 1024 * 1024
PIECE = 256
BUFFERS = 4
QUICK = pl.CostEstimate(flops=1024, bytes_accessed=1024, transcendentals=0)


def whole(shape):
    return pl.BlockSpec(shape, lambda *_: (0,) * len(shape))


def fold(scores, values_t, lo, at, acc, top, tot):
    span = pl.ds(lo, PIECE)
    old = top[pl.ds(at, 1), span]
    new = jnp.maximum(old, jnp.max(scores, axis=0, keepdims=True))
    expo = jnp.exp2(scores - new)
    keep = jnp.exp2(old - new)
    tot[pl.ds(at, 1), span] = tot[pl.ds(at, 1), span] * keep + jnp.sum(expo, axis=0, keepdims=True)
    top[pl.ds(at, 1), span] = new
    add = jnp.dot(values_t, expo.astype(BF16), preferred_element_type=F32)
    acc[at, :, span] = acc[at, :, span] * keep + add


def visit_kernel(first, tbl, meta, q_ref, *refs):
    if first:
        kv_ref, a_ref, b_ref, acc_out, top_out, tot_out, acc, top, tot, held, sems = refs
    else:
        acc_in, top_in, tot_in, a_ref, b_ref, out, acc, top, tot, held, sems, acc_was, acc_sem = refs
    width = HEADS * ROWS
    count = meta[0]

    def fetch(i):
        item = tbl[i]
        slot = i & (BUFFERS - 1)

        @pl.when(((item >> 5) & 1) == 1)
        def _():
            pltpu.make_async_copy(a_ref.at[item & 31], held.at[slot], sems.at[slot]).start()

        @pl.when(((item >> 5) & 1) == 0)
        def _():
            pltpu.make_async_copy(b_ref.at[item & 31], held.at[slot], sems.at[slot]).start()

    for i in range(BUFFERS - 1):
        pl.when(i < count)(functools.partial(fetch, i))

    if not first:
        pltpu.make_async_copy(acc_in, acc_was, acc_sem).start()
    acc[...] = jnp.zeros_like(acc)
    top[...] = jnp.full_like(top, MASKED)
    tot[...] = jnp.zeros_like(tot)
    if first:
        keys = kv_ref[:, :HD]
        values_t = kv_ref[:, HD:].astype(F32).T.astype(BF16)
        token = lax.broadcasted_iota(jnp.int32, (ROWS, PIECE), 0)
        row = lax.broadcasted_iota(jnp.int32, (ROWS, PIECE), 1) & (ROWS - 1)
        visible = (token <= row) & (token < meta[2])
        for lo in range(0, width, PIECE):
            scores = jnp.dot(keys, q_ref[meta[1], 0:HD, pl.ds(lo, PIECE)], preferred_element_type=F32)
            fold(jnp.where(visible, scores * SCALE, MASKED), values_t, lo, meta[1], acc, top, tot)

    def one(i, carry):
        slot = i & (BUFFERS - 1)
        pltpu.make_async_copy(a_ref.at[0], held.at[slot], sems.at[slot]).wait()
        ahead = i + BUFFERS - 1
        pl.when(ahead < count)(lambda: fetch(ahead))
        at = tbl[i] >> 6
        keys = held[slot, :, :HD]
        values_t = held[slot, :, HD:].astype(F32).T.astype(BF16)
        for lo in range(0, width, PIECE):
            scores = jnp.dot(keys, q_ref[at, 0:HD, pl.ds(lo, PIECE)], preferred_element_type=F32)
            fold(scores * SCALE, values_t, lo, at, acc, top, tot)
        return carry

    lax.fori_loop(0, count, one, 0)

    if first:
        acc_out[...] = acc[...]
        top_out[...] = top[...]
        tot_out[...] = tot[...]
    else:
        pltpu.make_async_copy(acc_in, acc_was, acc_sem).wait()
        line = lax.broadcasted_iota(jnp.int32, (16, width), 0)
        for k in range(NZ):
            row = slice(k, k + 1)
            both = jnp.maximum(top[row, :], top_in[row, :])
            keep, keep_was = jnp.exp2(top[row, :] - both), jnp.exp2(top_in[row, :] - both)
            total = tot[row, :] * keep + tot_in[row, :] * keep_was
            safe = jnp.where(total > 0, total, 1.0)
            keep, keep_was = keep / safe, keep_was / safe
            out[k, 0:HD, :] = (acc[k] * keep + acc_was[k] * keep_was).astype(BF16)
            weight = both + jnp.log2(safe)
            high = weight.astype(BF16).astype(F32)
            middle = (weight - high).astype(BF16).astype(F32)
            low = weight - high - middle
            stats = jnp.where(line == 0, high, jnp.where(line == 1, middle, jnp.where(line == 2, low, 0.0)))
            out[k, HD:, :] = stats.astype(BF16)


def visit(first, tbl, meta, q_t, given, pages_a, pages_b):
    width = HEADS * ROWS
    state = [(NZ, HD, width), (NZ, width), (NZ, width)]
    anywhere = pl.BlockSpec(memory_space=pl.ANY)
    scratch = [pltpu.VMEM(s, F32) for s in state]
    scratch += [pltpu.VMEM((BUFFERS, PAGE, 2 * HD), BF16), pltpu.SemaphoreType.DMA((BUFFERS,))]
    if first:
        out_shape = [jax.ShapeDtypeStruct(s, F32) for s in state]
        given_specs = [whole(given[0].shape)]
    else:
        out_shape = [jax.ShapeDtypeStruct((NZ, HD + 16, width), BF16)]
        given_specs = [anywhere, whole(given[1].shape), whole(given[2].shape)]
        scratch += [pltpu.VMEM(state[0], F32), pltpu.SemaphoreType.DMA]
    return pl.pallas_call(
        functools.partial(visit_kernel, first),
        grid_spec=pltpu.PrefetchScalarGridSpec(
            num_scalar_prefetch=2,
            grid=(1,),
            in_specs=[whole(q_t.shape)] + given_specs + [anywhere] * 2,
            out_specs=[whole(o.shape) for o in out_shape],
            scratch_shapes=scratch,
        ),
        out_shape=out_shape,
        compiler_params=pltpu.CompilerParams(vmem_limit_bytes=VMEM_LIMIT),
        cost_estimate=QUICK,
    )(tbl, meta, q_t, *given, pages_a, pages_b)


def carry_kernel(n, tbl, pick, c_ref, *refs):
    pages, out = refs[: 4 * n], refs[4 * n]
    k = pl.program_id(0)
    for slot in range(4):
        page = pages[slot * n][0]
        if n == 2:
            page = jnp.where(pick[k * 4 + slot] == 0, page, pages[slot * n + 1][0])
        out[0, slot] = lax.dot_general(
            c_ref[0], page, (((1,), (1,)), ((), ())), preferred_element_type=F32
        ).astype(BF16)


def carry(tbl, pick, shift, c_rows, sources):
    n = len(sources[0])
    specs, given = [], []

    def where(slot, part, size):
        def index(k, tbl, pick):
            here = pick[k * 4 + slot] == part
            return (jnp.where(here, tbl[k * 4 + slot], 0), 0, 0)

        return pl.BlockSpec((1, PAGE, NS), index)

    for slot in range(4):
        for part in range(n):
            given.append(sources[slot // 2][part])
            specs.append(where(slot, part, given[-1].shape[0]))
    return pl.pallas_call(
        functools.partial(carry_kernel, n),
        grid_spec=pltpu.PrefetchScalarGridSpec(
            num_scalar_prefetch=2,
            grid=(NZ,),
            in_specs=[pl.BlockSpec((1, ROWS, NS), lambda k, tbl, pick: (k, 0, 0))] + specs,
            out_specs=pl.BlockSpec((1, 4, ROWS, PAGE), lambda k, tbl, pick: (k, 0, 0, 0)),
        ),
        out_shape=jax.ShapeDtypeStruct((NZ, 4, ROWS, PAGE), BF16),
        compiler_params=pltpu.CompilerParams(vmem_limit_bytes=VMEM_LIMIT),
        cost_estimate=QUICK,
    )(tbl, pick, c_rows, *given)


def join_kernel(length, *refs):
    ref, out = refs
    parts = [ref.at[k] for k in range(NZ)]
    stats = [p[HD : HD + 16, :].astype(F32) for p in parts]
    weights = [s[0:1] + s[1:2] + s[2:3] for s in stats]
    top = functools.reduce(jnp.maximum, weights)
    weights = [jnp.exp2(w - top) for w in weights]
    row = lax.broadcasted_iota(jnp.int32, (1, HEADS * ROWS), 1) & (ROWS - 1)
    scale = jnp.where(row < length[0], 1.0 / functools.reduce(jnp.add, weights), 0.0)
    weights = [w * scale for w in weights]
    for head in range(HEADS):
        span = pl.ds(head * ROWS, ROWS)
        total = sum(
            p[0:HD, span].astype(F32) * w[:, head * ROWS : (head + 1) * ROWS]
            for p, w in zip(parts, weights)
        )
        out[:, span] = total.T.astype(BF16)


def join(length, parts):
    return pl.pallas_call(
        join_kernel,
        grid_spec=pltpu.PrefetchScalarGridSpec(
            num_scalar_prefetch=1,
            grid=(1,),
            in_specs=[whole(parts.shape)],
            out_specs=whole((ROWS, HEADS * HD)),
        ),
        out_shape=jax.ShapeDtypeStruct((ROWS, HEADS * HD), BF16),
        compiler_params=pltpu.CompilerParams(vmem_limit_bytes=VMEM_LIMIT),
        cost_estimate=QUICK,
    )(length, parts)


def inner_kernel(
    x_ref, z_ref, b_ref, c_ref, cum_ref, cum_t_ref, dt_t_ref, skip_ref, base_ref, grown_ref, gate_ref, products
):
    heads = cum_ref.shape[2]
    width = x_ref.shape[1]

    @pl.when(pl.program_id(0) == 0)
    def _():
        products[...] = lax.dot_general(
            c_ref[...], b_ref[...], (((1,), (1,)), ((), ())), preferred_element_type=F32
        )

    x = x_ref[...].astype(F32)
    causal = lax.broadcasted_iota(jnp.int32, (ROWS, ROWS), 0) >= lax.broadcasted_iota(jnp.int32, (ROWS, ROWS), 1)
    head_of = lax.broadcasted_iota(jnp.int32, (ROWS, width), 1) >> 6
    within = jnp.zeros((ROWS, width), F32)
    grown = jnp.zeros((ROWS, width), F32)
    for head in range(heads):
        column = cum_ref[0, :, head : head + 1]
        spread = jnp.where(causal, column - cum_t_ref[0, head : head + 1, :], MASKED)
        mixing = jnp.exp(spread) * products[...] * dt_t_ref[0, head : head + 1, :]
        mine = jnp.where(head_of == head, x, 0.0).astype(BF16)
        within += jnp.dot(mixing.astype(BF16), mine, preferred_element_type=F32)
        grown = jnp.where(head_of == head, jnp.exp(column), grown)
    gate = z_ref[...].astype(F32)
    base_ref[...] = within + skip_ref[...] * x
    grown_ref[...] = grown
    gate_ref[...] = gate / (1.0 + jnp.exp(-gate))


def inner(x, z, b, c, cum, dt, d_skip):
    heads = cum.shape[1] // SP
    width = x.shape[1] // SP
    cum4 = cum.reshape(ROWS, SP, heads).transpose(1, 0, 2)
    cum_t = cum.T.reshape(SP, heads, ROWS)
    dt_t = dt.T.reshape(SP, heads, ROWS)
    skip = jnp.repeat(d_skip, width // heads)[None]
    columns = pl.BlockSpec((ROWS, width), lambda i: (0, i))
    stack = lambda *s: pl.BlockSpec((1,) + s, lambda i: (i, 0, 0))
    return pl.pallas_call(
        inner_kernel,
        grid=(SP,),
        in_specs=[
            columns,
            columns,
            whole(b.shape),
            whole(c.shape),
            stack(ROWS, heads),
            stack(heads, ROWS),
            stack(heads, ROWS),
            pl.BlockSpec((1, width), lambda i: (0, i)),
        ],
        out_specs=[columns] * 3,
        scratch_shapes=[pltpu.VMEM((ROWS, ROWS), F32)],
        out_shape=[jax.ShapeDtypeStruct(x.shape, F32)] * 3,
        compiler_params=pltpu.CompilerParams(vmem_limit_bytes=VMEM_LIMIT),
        cost_estimate=QUICK,
    )(x, z, b, c, cum4, cum_t, dt_t, skip)


def finish_kernel(where, pick, length, base_ref, grown_ref, gate_ref, gain_ref, near_ref, far_ref, out_ref, gated, squares):
    step = pl.program_id(0)
    width = base_ref.shape[1]

    @pl.when(step == 0)
    def _():
        squares[...] = jnp.zeros_like(squares)

    got = jnp.where(pick[step] == 0, near_ref[0], far_ref[0]).astype(F32)
    value = (base_ref[...] + grown_ref[...] * got) * gate_ref[...]
    gated[step] = value
    squares[...] += value * value

    @pl.when(step == pl.num_programs(0) - 1)
    def _():
        mean = jnp.sum(squares[...], axis=1, keepdims=True) / (SP * PAGE)
        row = lax.broadcasted_iota(jnp.int32, (ROWS, 1), 0)
        scale = jnp.where(row < length[0], lax.rsqrt(mean + 1e-05), 0.0)
        for part in range(SP):
            span = slice(part * width, (part + 1) * width)
            out_ref[:, span] = (gated[part] * scale * gain_ref[:, span]).astype(BF16)


def finish(where, pick, length, base, grown, gate, gain, near, far):
    width = base.shape[1] // SP
    columns = pl.BlockSpec((ROWS, width), lambda i, w, p, n: (0, i))

    def block(chosen):
        return pl.BlockSpec((1, ROWS, width), lambda i, w, p, n: (jnp.where(p[i] == chosen, w[i], 0), 0, 0))

    return pl.pallas_call(
        finish_kernel,
        grid_spec=pltpu.PrefetchScalarGridSpec(
            num_scalar_prefetch=3,
            grid=(SP,),
            in_specs=[columns] * 3 + [whole((1, SP * width)), block(0), block(1)],
            out_specs=whole((ROWS, SP * width)),
            scratch_shapes=[pltpu.VMEM((SP, ROWS, width), F32), pltpu.VMEM((ROWS, width), F32)],
        ),
        out_shape=jax.ShapeDtypeStruct((ROWS, SP * width), BF16),
        compiler_params=pltpu.CompilerParams(vmem_limit_bytes=VMEM_LIMIT),
        cost_estimate=QUICK,
    )(where, pick, length, base, grown, gate, gain[None], near, far)


def listing(chosen, value):
    place = jnp.cumsum(chosen.astype(jnp.int32)) - 1
    slot = jnp.arange(VISITS)[:, None]
    hot = chosen[None, :] & (place[None, :] == slot)
    return jnp.sum(jnp.where(hot, value[None, :], 0), axis=1), jnp.sum(chosen.astype(jnp.int32))


def ranks(owners):
    order = jnp.arange(owners.shape[-1])
    earlier = order[None, :] < order[:, None]
    same = owners[..., :, None] == owners[..., None, :]
    return jnp.sum((same & earlier).astype(jnp.int32), axis=-1)


def tie(*trees):
    return lax.optimization_barrier(trees)


def shards(
    queries, kv_new, page_pool, hit_owner, hit_page, prefix_blocks, suffix_len, out_weight,
    mamba_x, mamba_z, mamba_b, mamba_c, mamba_dt, a_log, d_skip, norm_gain,
):
    me_x, me_z, me_c = lax.axis_index("xl"), lax.axis_index("z"), lax.axis_index("co")
    me_t = lax.axis_index(("y", "xh"))
    swap = [(0, 1), (1, 0)]

    far = lax.ppermute(page_pool, "xl", swap)
    own_b = lax.ppermute(page_pool, "co", swap)
    numbers = jnp.concatenate([hit_owner[0], hit_page[0], prefix_blocks]).astype(BF16)
    packed = jnp.concatenate([mamba_c, jnp.pad(numbers[None, :], ((0, 15), (0, NS - numbers.shape[0])))], axis=0)
    shared = lax.all_to_all(jnp.broadcast_to(packed[None], (NZ,) + packed.shape), "z", 0, 0, tiled=True)
    q_t = queries.reshape(ROWS, HEADS, HD).transpose(2, 1, 0).reshape(HD, HEADS * ROWS)
    q_all = lax.all_gather(q_t, "z", axis=0, tiled=False)

    table = shared[:, ROWS, : 2 * HITS + 1].astype(jnp.int32)
    owners, page_ids, live = table[:, :HITS], table[:, HITS : 2 * HITS], table[:, 2 * HITS]
    mine = (owners // 2) % NZ == me_z
    near = owners // 16 == me_x
    same_core = owners % 2 == me_c
    request = jnp.broadcast_to(jnp.arange(NZ)[:, None], owners.shape)
    wanted = mine & (jnp.arange(HITS)[None, :] < jnp.minimum(live, PMAX)[:, None])

    def listed(chosen, ids):
        value = ids + 32 * same_core.astype(jnp.int32) + 64 * request
        flat = lambda a: a[:, :PMAX].reshape(-1)
        tbl, count = listing(flat(wanted & chosen), flat(value))
        return tbl, jnp.stack([count, me_z, suffix_len[0]])

    tbl_near, meta_near = listed(near, page_ids)
    tbl_far, meta_far = listed(~near, page_ids)

    held, held_ids = owners[:, PMAX:], page_ids[:, PMAX:]
    held_slot = 2 * (held % 2 != me_c).astype(jnp.int32) + ranks(held)

    def slots(chosen):
        hot = chosen[:, None, :] & (held_slot[:, None, :] == jnp.arange(4)[None, :, None])
        return jnp.sum(jnp.where(hot, held_ids[:, None, :], 0), axis=2).reshape(-1)

    c_rows = shared[:, :ROWS]
    held_here = mine[:, PMAX:]
    held_near = near[:, PMAX:]
    ids_near = slots(held_here & held_near)
    ids_far = slots(held_here & ~held_near)
    none = jnp.zeros_like(ids_near)
    sent_near = carry(ids_near, none, me_z, c_rows, [[page_pool], [own_b]])
    got_near = lax.all_to_all(sent_near, "z", 0, 0, tiled=True)

    cum = jnp.cumsum(-jnp.exp(a_log)[None, :] * mamba_dt, axis=0)
    base, grown, gate = inner(mamba_x, mamba_z, mamba_b, mamba_c, cum, mamba_dt, d_skip)
    q_all, got_near, base = tie(q_all, got_near, base)
    state = visit(True, tbl_near, meta_near, q_all, [kv_new], page_pool, own_b)
    far, state = tie(far, state)
    far_b = lax.ppermute(far, "co", swap)
    (parts,) = visit(False, tbl_far, meta_far, q_all, state, far, far_b)
    c_rows, out_weight, parts = tie(c_rows, out_weight, parts)
    parts = lax.all_to_all(parts, "z", 0, 0, tiled=True)
    sent_far = carry(ids_far, none, me_z, c_rows, [[far], [far_b]])

    attn_out = join(suffix_len, parts)
    weight = lax.all_gather(out_weight, ("xl", "co"), axis=1, tiled=True)
    attn_out, weight = tie(attn_out, weight)
    gathered = lax.all_gather(attn_out, "z", axis=0, tiled=True)
    gathered, sent_far = tie(gathered, sent_far)
    got_far = lax.all_to_all(sent_far, "z", 0, 0, tiled=True)
    partial = jnp.dot(gathered, weight, preferred_element_type=F32).astype(BF16)
    partial = partial.reshape(NZ, ROWS, -1)
    total = lax.dynamic_index_in_dim(partial, me_t, 0, keepdims=False).astype(F32)
    for k in range(1, NTP):
        piece = lax.dynamic_index_in_dim(partial, me_t ^ k, 0, keepdims=False)
        total += lax.ppermute(piece, ("y", "xh"), [(i, i ^ k) for i in range(NTP)]).astype(F32)
    total = total.astype(BF16)
    total, got_far = tie(total, got_far)
    half = total.shape[1] // 2
    arrived = []
    for k in range(2):
        piece = jnp.where((me_z % 2) ^ k == 0, total[:, :half], total[:, half:])
        pairs = []
        for z in range(NZ):
            for t in range(NTP):
                goal = 4 * ((z % 2) ^ k) + z // 2
                pairs.append((z * NTP + t, t * NTP + goal))
        arrived.append(lax.ppermute(piece, ("z", "y", "xh"), pairs))
    swapped = me_t // 4 == 1
    attn_proj = jnp.concatenate(
        [jnp.where(swapped, arrived[1], arrived[0]), jnp.where(swapped, arrived[0], arrived[1])], axis=1
    )

    from_owner = hit_owner[0, PMAX:]
    slot = 2 * (from_owner % 2 != me_c).astype(jnp.int32) + ranks(from_owner)
    where = (from_owner // 2) % NZ * 4 + slot
    pick = (from_owner // 16 != me_x).astype(jnp.int32)
    flat = lambda a: a.reshape(4 * NZ, ROWS, PAGE)
    mamba_out = finish(where, pick, suffix_len, base, grown, gate, norm_gain, flat(got_near), flat(got_far))
    return (attn_proj, mamba_out)


def solution(mesh):
    fine = Mesh(mesh.devices.reshape(2, 8, 2, 4, 2), ("xl", "z", "co", "y", "xh"))
    store, tp = ("xl", "z", "co"), ("y", "xh")
    both = P(store, tp)
    specs = (
        both, both, P(store, None, tp), P(store, None), P(store, None), P(store), P(store), P(tp, store),
        both, both, both, both, both, P(tp), P(tp), P(tp),
    )
    return jax.shard_map(shards, mesh=fine, in_specs=specs, out_specs=(both, both), check_vma=False)
```

```python
import functools

import jax
import jax.numpy as jnp
from jax import lax
from jax.experimental import pallas as pl
from jax.experimental.pallas import tpu as pltpu
from jax.sharding import Mesh, PartitionSpec as P

HD = 128
HEADS = 8
NS = 256
PAGE = 256
SP = 8
CAP = 2
PMAX = 28
HITS = 36
POOL = 32
ROWS = 128
NZ = 8
NTP = 8
VISITS = 32
MASKED = -1e30
SCALE = HD ** (-0.5) * 1.4426950408889634
F32 = jnp.float32
BF16 = jnp.bfloat16
VMEM_LIMIT = 60 * 1024 * 1024
PIECE = 256
TALL = HD + 16
LANES = 128
QUICK = pl.CostEstimate(flops=1024, bytes_accessed=1024, transcendentals=0)


def whole(shape):
    return pl.BlockSpec(shape, lambda *_: (0,) * len(shape))


def product(keys, q_ref, at):
    return [
        jnp.dot(keys, q_ref[at, :, pl.ds(lo, PIECE)], preferred_element_type=F32)
        for lo in range(0, HEADS * ROWS, PIECE)
    ]


def values(block):
    turned = block.astype(F32).T.astype(BF16)
    return jnp.concatenate([turned, jnp.ones((TALL - HD, block.shape[0]), BF16)], axis=0)


def absorb(pieces, values_t, at, shift, acc, top):
    for lo, raw in zip(range(0, HEADS * ROWS, PIECE), pieces):
        span = pl.ds(lo, PIECE)
        old = top[pl.ds(at, 1), span]
        new = jnp.maximum(old, jnp.max(raw, axis=0, keepdims=True) * SCALE + shift)
        expo = jnp.exp2(raw * SCALE - (new - shift))
        keep = jnp.exp2(old - new)
        top[pl.ds(at, 1), span] = new
        add = jnp.dot(values_t, expo.astype(BF16), preferred_element_type=F32)
        acc[at, :, span] = acc[at, :, span] * keep + add


def visit_kernel(first, tbl, meta, q_ref, *refs):
    if first:
        kv_ref, a_ref, b_ref, acc_out, top_out, acc, top, held, sems = refs
    else:
        acc_in, top_in, a_ref, b_ref, *outs, acc, top, held, sems, acc_was, acc_sem = refs
    width = HEADS * ROWS
    count = meta[0]
    turns = (count + 1) >> 1

    def fetch(turn):
        for side in range(2):
            item = tbl[turn * 2 + side]
            slot = (turn & 1) * 2 + side

            @pl.when(((item >> 5) & 1) == 1)
            def _():
                pltpu.make_async_copy(a_ref.at[item & 31], held.at[slot], sems.at[slot]).start()

            @pl.when(((item >> 5) & 1) == 0)
            def _():
                pltpu.make_async_copy(b_ref.at[item & 31], held.at[slot], sems.at[slot]).start()

    pl.when(turns > 0)(lambda: fetch(0))
    if not first:
        pltpu.make_async_copy(acc_in, acc_was, acc_sem).start()
    acc[...] = jnp.zeros_like(acc)
    top[...] = jnp.full_like(top, MASKED)
    if first:
        token = lax.broadcasted_iota(jnp.int32, (ROWS, PIECE), 0)
        row = lax.broadcasted_iota(jnp.int32, (ROWS, PIECE), 1) & (ROWS - 1)
        visible = (token <= row) & (token < meta[2])
        pieces = [jnp.where(visible, raw, MASKED) for raw in product(kv_ref[:, :HD], q_ref, meta[1])]
        absorb(pieces, values(kv_ref[:, HD:]), meta[1], 0.0, acc, top)

    def one(turn, carry):
        base = (turn & 1) * 2
        for side in range(2):
            pltpu.make_async_copy(a_ref.at[0], held.at[base + side], sems.at[base + side]).wait()
        pl.when(turn + 1 < turns)(lambda: fetch(turn + 1))
        places = [tbl[turn * 2 + side] >> 6 for side in range(2)]
        pieces = [product(held[base + side, :, :HD], q_ref, places[side]) for side in range(2)]
        values_t = [values(held[base + side, :, HD:]) for side in range(2)]
        absent = jnp.where(turn * 2 + 1 < count, 0.0, 2 * MASKED)
        absorb(pieces[0], values_t[0], places[0], 0.0, acc, top)
        absorb(pieces[1], values_t[1], places[1], absent, acc, top)
        return carry

    lax.fori_loop(0, turns, one, 0)

    if first:
        acc_out[...] = acc[...]
        top_out[...] = top[...]
    else:
        pltpu.make_async_copy(acc_in, acc_was, acc_sem).wait()
        line = lax.broadcasted_iota(jnp.int32, (16, width), 0)
        for k, out in enumerate(outs):
            at = (meta[1] + k) & (NZ - 1)
            row = pl.ds(at, 1)
            now, was = top[row, :], top_in[row, :]
            both = jnp.maximum(now, was)
            keep, keep_was = jnp.exp2(now - both), jnp.exp2(was - both)
            total = acc[at, HD : HD + 1, :] * keep + acc_was[at, HD : HD + 1, :] * keep_was
            safe = jnp.where(total > 0, total, 1.0)
            keep, keep_was = keep / safe, keep_was / safe
            out[0:HD, :] = (acc[at, 0:HD, :] * keep + acc_was[at, 0:HD, :] * keep_was).astype(BF16)
            weight = both + jnp.log2(safe)
            high = weight.astype(BF16).astype(F32)
            middle = (weight - high).astype(BF16).astype(F32)
            low = weight - high - middle
            stats = jnp.where(line == 0, high, jnp.where(line == 1, middle, jnp.where(line == 2, low, 0.0)))
            out[HD:, :] = stats.astype(BF16)


def visit(first, tbl, meta, q_t, given, pages_a, pages_b):
    width = HEADS * ROWS
    state = [(NZ, TALL, width), (NZ, width)]
    anywhere = pl.BlockSpec(memory_space=pl.ANY)
    scratch = [pltpu.VMEM(s, F32) for s in state]
    scratch += [pltpu.VMEM((4, PAGE, 2 * HD), BF16), pltpu.SemaphoreType.DMA((4,))]
    if first:
        out_shape = [jax.ShapeDtypeStruct(s, F32) for s in state]
        given_specs = [whole(given[0].shape)]
    else:
        out_shape = [jax.ShapeDtypeStruct((HD + 16, width), BF16)] * NZ
        given_specs = [anywhere, whole(given[1].shape)]
        scratch += [pltpu.VMEM(state[0], F32), pltpu.SemaphoreType.DMA]
    return pl.pallas_call(
        functools.partial(visit_kernel, first),
        grid_spec=pltpu.PrefetchScalarGridSpec(
            num_scalar_prefetch=2,
            grid=(1,),
            in_specs=[whole(q_t.shape)] + given_specs + [anywhere] * 2,
            out_specs=[whole(o.shape) for o in out_shape],
            scratch_shapes=scratch,
        ),
        out_shape=out_shape,
        compiler_params=pltpu.CompilerParams(vmem_limit_bytes=VMEM_LIMIT),
        cost_estimate=QUICK,
    )(tbl, meta, q_t, *given, pages_a, pages_b)


def carry_kernel(n, tbl, pick, c_ref, *refs):
    pages, out = refs[: 4 * n], refs[4 * n]
    k = pl.program_id(0)
    for slot in range(4):
        page = pages[slot * n][0]
        if n == 2:
            page = jnp.where(pick[k * 4 + slot] == 0, page, pages[slot * n + 1][0])
        out[0, slot] = lax.dot_general(
            c_ref[0], page, (((1,), (1,)), ((), ())), preferred_element_type=F32
        ).astype(BF16)


def carry(tbl, pick, shift, c_rows, sources):
    n = len(sources[0])
    specs, given = [], []

    def where(slot, part, size):
        def index(k, tbl, pick):
            here = pick[k * 4 + slot] == part
            return (jnp.where(here, tbl[k * 4 + slot], 0), 0, 0)

        return pl.BlockSpec((1, PAGE, NS), index)

    for slot in range(4):
        for part in range(n):
            given.append(sources[slot // 2][part])
            specs.append(where(slot, part, given[-1].shape[0]))
    return pl.pallas_call(
        functools.partial(carry_kernel, n),
        grid_spec=pltpu.PrefetchScalarGridSpec(
            num_scalar_prefetch=2,
            grid=(NZ,),
            in_specs=[pl.BlockSpec((1, ROWS, NS), lambda k, tbl, pick: (k, 0, 0))] + specs,
            out_specs=pl.BlockSpec((1, 4, ROWS, PAGE), lambda k, tbl, pick: (k, 0, 0, 0)),
        ),
        out_shape=jax.ShapeDtypeStruct((NZ, 4, ROWS, PAGE), BF16),
        compiler_params=pltpu.CompilerParams(vmem_limit_bytes=VMEM_LIMIT),
        cost_estimate=QUICK,
    )(tbl, pick, c_rows, *given)


def join_kernel(length, *refs):
    parts, out = refs[:NZ], refs[NZ]
    stats = [p[HD : HD + 16, :].astype(F32) for p in parts]
    weights = [s[0:1] + s[1:2] + s[2:3] for s in stats]
    top = functools.reduce(jnp.maximum, weights)
    weights = [jnp.exp2(w - top) for w in weights]
    row = lax.broadcasted_iota(jnp.int32, (1, HEADS * ROWS), 1) & (ROWS - 1)
    scale = jnp.where(row < length[0], 1.0 / functools.reduce(jnp.add, weights), 0.0)
    weights = [w * scale for w in weights]
    for head in range(HEADS):
        span = pl.ds(head * ROWS, ROWS)
        total = sum(
            p[0:HD, span].astype(F32) * w[:, head * ROWS : (head + 1) * ROWS]
            for p, w in zip(parts, weights)
        )
        out[:, span] = total.T.astype(BF16)


def join(length, parts):
    return pl.pallas_call(
        join_kernel,
        grid_spec=pltpu.PrefetchScalarGridSpec(
            num_scalar_prefetch=1,
            grid=(1,),
            in_specs=[whole(p.shape) for p in parts],
            out_specs=whole((ROWS, HEADS * HD)),
        ),
        out_shape=jax.ShapeDtypeStruct((ROWS, HEADS * HD), BF16),
        compiler_params=pltpu.CompilerParams(vmem_limit_bytes=VMEM_LIMIT),
        cost_estimate=QUICK,
    )(length, *parts)


def inner_kernel(
    x_ref, z_ref, b_ref, c_ref, cum_ref, cum_t_ref, dt_t_ref, skip_ref, base_ref, grown_ref, gate_ref, products
):
    heads = cum_ref.shape[2]
    width = x_ref.shape[1]

    @pl.when(pl.program_id(0) == 0)
    def _():
        products[...] = lax.dot_general(
            c_ref[...], b_ref[...], (((1,), (1,)), ((), ())), preferred_element_type=F32
        )

    x = x_ref[...].astype(F32)
    causal = lax.broadcasted_iota(jnp.int32, (ROWS, ROWS), 0) >= lax.broadcasted_iota(jnp.int32, (ROWS, ROWS), 1)
    head_of = lax.broadcasted_iota(jnp.int32, (ROWS, width), 1) >> 6
    within = jnp.zeros((ROWS, width), F32)
    grown = jnp.zeros((ROWS, width), F32)
    for head in range(heads):
        column = cum_ref[0, :, head : head + 1]
        spread = jnp.where(causal, column - cum_t_ref[0, head : head + 1, :], MASKED)
        mixing = jnp.exp(spread) * products[...] * dt_t_ref[0, head : head + 1, :]
        mine = jnp.where(head_of == head, x, 0.0).astype(BF16)
        within += jnp.dot(mixing.astype(BF16), mine, preferred_element_type=F32)
        grown = jnp.where(head_of == head, jnp.exp(column), grown)
    gate = z_ref[...].astype(F32)
    base_ref[...] = within + skip_ref[...] * x
    grown_ref[...] = grown
    gate_ref[...] = gate / (1.0 + jnp.exp(-gate))


def inner(x, z, b, c, cum, dt, d_skip):
    heads = cum.shape[1] // SP
    width = x.shape[1] // SP
    cum4 = cum.reshape(ROWS, SP, heads).transpose(1, 0, 2)
    cum_t = cum.T.reshape(SP, heads, ROWS)
    dt_t = dt.T.reshape(SP, heads, ROWS)
    skip = jnp.repeat(d_skip, width // heads)[None]
    columns = pl.BlockSpec((ROWS, width), lambda i: (0, i))
    stack = lambda *s: pl.BlockSpec((1,) + s, lambda i: (i, 0, 0))
    return pl.pallas_call(
        inner_kernel,
        grid=(SP,),
        in_specs=[
            columns,
            columns,
            whole(b.shape),
            whole(c.shape),
            stack(ROWS, heads),
            stack(heads, ROWS),
            stack(heads, ROWS),
            pl.BlockSpec((1, width), lambda i: (0, i)),
        ],
        out_specs=[columns] * 3,
        scratch_shapes=[pltpu.VMEM((ROWS, ROWS), F32)],
        out_shape=[jax.ShapeDtypeStruct(x.shape, F32)] * 3,
        compiler_params=pltpu.CompilerParams(vmem_limit_bytes=VMEM_LIMIT),
        cost_estimate=QUICK,
    )(x, z, b, c, cum4, cum_t, dt_t, skip)


def finish_kernel(where, pick, length, base_ref, grown_ref, gate_ref, gain_ref, near_ref, far_ref, out_ref, gated, squares):
    step = pl.program_id(0)
    width = base_ref.shape[1]

    @pl.when(step == 0)
    def _():
        squares[...] = jnp.zeros_like(squares)

    got = jnp.where(pick[step] == 0, near_ref[0], far_ref[0]).astype(F32)
    value = (base_ref[...] + grown_ref[...] * got) * gate_ref[...]
    gated[step] = value
    squares[...] += value * value

    @pl.when(step == pl.num_programs(0) - 1)
    def _():
        mean = jnp.sum(squares[...], axis=1, keepdims=True) / (SP * PAGE)
        row = lax.broadcasted_iota(jnp.int32, (ROWS, 1), 0)
        scale = jnp.where(row < length[0], lax.rsqrt(mean + 1e-05), 0.0)
        for part in range(SP):
            span = slice(part * width, (part + 1) * width)
            out_ref[:, span] = (gated[part] * scale * gain_ref[:, span]).astype(BF16)


def finish(where, pick, length, base, grown, gate, gain, near, far):
    width = base.shape[1] // SP
    columns = pl.BlockSpec((ROWS, width), lambda i, w, p, n: (0, i))

    def block(chosen):
        return pl.BlockSpec((1, ROWS, width), lambda i, w, p, n: (jnp.where(p[i] == chosen, w[i], 0), 0, 0))

    return pl.pallas_call(
        finish_kernel,
        grid_spec=pltpu.PrefetchScalarGridSpec(
            num_scalar_prefetch=3,
            grid=(SP,),
            in_specs=[columns] * 3 + [whole((1, SP * width)), block(0), block(1)],
            out_specs=whole((ROWS, SP * width)),
            scratch_shapes=[pltpu.VMEM((SP, ROWS, width), F32), pltpu.VMEM((ROWS, width), F32)],
        ),
        out_shape=jax.ShapeDtypeStruct((ROWS, SP * width), BF16),
        compiler_params=pltpu.CompilerParams(vmem_limit_bytes=VMEM_LIMIT),
        cost_estimate=QUICK,
    )(where, pick, length, base, grown, gate, gain[None], near, far)


def listing(chosen, value):
    place = jnp.cumsum(chosen.astype(jnp.int32)) - 1
    slot = jnp.arange(VISITS)[:, None]
    hot = chosen[None, :] & (place[None, :] == slot)
    return jnp.sum(jnp.where(hot, value[None, :], 0), axis=1), jnp.sum(chosen.astype(jnp.int32))


def ranks(owners):
    order = jnp.arange(owners.shape[-1])
    earlier = order[None, :] < order[:, None]
    same = owners[..., :, None] == owners[..., None, :]
    return jnp.sum((same & earlier).astype(jnp.int32), axis=-1)


def tie(*trees):
    return lax.optimization_barrier(trees)


def shards(
    queries, kv_new, page_pool, hit_owner, hit_page, prefix_blocks, suffix_len, out_weight,
    mamba_x, mamba_z, mamba_b, mamba_c, mamba_dt, a_log, d_skip, norm_gain,
):
    me_x, me_z, me_c = lax.axis_index("xl"), lax.axis_index("z"), lax.axis_index("co")
    me_t = lax.axis_index(("y", "xh"))
    swap = [(0, 1), (1, 0)]

    far = lax.ppermute(page_pool, "xl", swap)
    own_b = lax.ppermute(page_pool, "co", swap)
    numbers = jnp.concatenate([hit_owner[0], hit_page[0], prefix_blocks]).astype(BF16)
    packed = jnp.concatenate([mamba_c, jnp.pad(numbers[None, :], ((0, 15), (0, NS - numbers.shape[0])))], axis=0)
    shared = lax.all_to_all(jnp.broadcast_to(packed[None], (NZ,) + packed.shape), "z", 0, 0, tiled=True)
    q_t = queries.reshape(ROWS, HEADS, HD).transpose(2, 1, 0).reshape(HD, HEADS * ROWS)
    q_all = lax.all_gather(q_t, "z", axis=0, tiled=False)

    table = shared[:, ROWS, : 2 * HITS + 1].astype(jnp.int32)
    owners, page_ids, live = table[:, :HITS], table[:, HITS : 2 * HITS], table[:, 2 * HITS]
    mine = (owners // 2) % NZ == me_z
    near = owners // 16 == me_x
    same_core = owners % 2 == me_c
    request = jnp.broadcast_to(jnp.arange(NZ)[:, None], owners.shape)
    wanted = mine & (jnp.arange(HITS)[None, :] < jnp.minimum(live, PMAX)[:, None])

    def listed(chosen, ids):
        value = ids + 32 * same_core.astype(jnp.int32) + 64 * request
        flat = lambda a: a[:, :PMAX].reshape(-1)
        tbl, count = listing(flat(wanted & chosen), flat(value))
        return tbl, jnp.stack([count, me_z, suffix_len[0]])

    tbl_near, meta_near = listed(near, page_ids)
    tbl_far, meta_far = listed(~near, page_ids)

    held, held_ids = owners[:, PMAX:], page_ids[:, PMAX:]
    held_slot = 2 * (held % 2 != me_c).astype(jnp.int32) + ranks(held)

    def slots(chosen):
        hot = chosen[:, None, :] & (held_slot[:, None, :] == jnp.arange(4)[None, :, None])
        return jnp.sum(jnp.where(hot, held_ids[:, None, :], 0), axis=2).reshape(-1)

    c_rows = shared[:, :ROWS]
    held_here = mine[:, PMAX:]
    held_near = near[:, PMAX:]
    ids_near = slots(held_here & held_near)
    ids_far = slots(held_here & ~held_near)
    none = jnp.zeros_like(ids_near)
    sent_near = carry(ids_near, none, me_z, c_rows, [[page_pool], [own_b]])
    got_near = lax.all_to_all(sent_near, "z", 0, 0, tiled=True)

    cum = jnp.cumsum(-jnp.exp(a_log)[None, :] * mamba_dt, axis=0)
    base, grown, gate = inner(mamba_x, mamba_z, mamba_b, mamba_c, cum, mamba_dt, d_skip)
    q_all, base = tie(q_all, base)
    state = visit(True, tbl_near, meta_near, q_all, [kv_new], page_pool, own_b)
    far, got_near, state = tie(far, got_near, state)
    far_b = lax.ppermute(far, "co", swap)
    parts = visit(False, tbl_far, meta_far, q_all, state, far, far_b)
    out_weight, far = tie(out_weight, far)
    pieces = []
    upper = me_z // 4
    for k in range(2):
        piece = jnp.where(upper == k, out_weight[:, :LANES], out_weight[:, LANES:])
        pairs = []
        for z in range(NZ):
            for core in range(2):
                goal = 4 * (z % 2) + 2 * core + ((z // 4) ^ k)
                pairs.append((z * 2 + core, goal * 2 + (z // 2) % 2))
        pieces.append(lax.ppermute(piece, ("z", "co"), pairs))
    c_rows, pieces, parts = tie(c_rows, pieces, parts)
    parts = [
        a if k == 0 else lax.ppermute(a, "z", [(i, (i + k) % NZ) for i in range(NZ)])
        for k, a in enumerate(parts)
    ]
    sent_far = carry(ids_far, none, me_z, c_rows, [[far], [far_b]])

    attn_out = join(suffix_len, parts)
    odd = me_z % 2 == 1
    halves = jnp.stack([jnp.where(odd, pieces[1], pieces[0]), jnp.where(odd, pieces[0], pieces[1])])
    weight = lax.all_gather(halves, ("xl", "co"), axis=0, tiled=True)
    attn_out, weight = tie(attn_out, weight)
    gathered = lax.all_gather(attn_out, "z", axis=0, tiled=True)
    gathered, sent_far = tie(gathered, sent_far)
    got_far = lax.all_to_all(sent_far, "z", 0, 0, tiled=True)
    def product_for(t):
        block = lax.dynamic_index_in_dim(weight, (t // 4) * 4 + (t % 2) * 2 + (t // 2) % 2, 0, keepdims=False)
        return jnp.dot(gathered, block, preferred_element_type=F32)

    total = product_for(me_t)
    for k in range(1, NTP):
        sent = product_for(me_t ^ k).astype(BF16)
        total += lax.ppermute(sent, ("y", "xh"), [(i, i ^ k) for i in range(NTP)]).astype(F32)
    total, got_far = tie(total.astype(BF16), got_far)
    columns = lax.all_to_all(total.reshape(NZ, ROWS, LANES), "z", 0, 0, tiled=True)
    attn_proj = columns.transpose(1, 0, 2).reshape(ROWS, NZ * LANES)

    from_owner = hit_owner[0, PMAX:]
    slot = 2 * (from_owner % 2 != me_c).astype(jnp.int32) + ranks(from_owner)
    where = (from_owner // 2) % NZ * 4 + slot
    pick = (from_owner // 16 != me_x).astype(jnp.int32)
    flat = lambda a: a.reshape(4 * NZ, ROWS, PAGE)
    mamba_out = finish(where, pick, suffix_len, base, grown, gate, norm_gain, flat(got_near), flat(got_far))
    return (attn_proj, mamba_out)


def solution(mesh):
    fine = Mesh(mesh.devices.reshape(2, 8, 2, 4, 2), ("xl", "z", "co", "y", "xh"))
    store, tp = ("xl", "z", "co"), ("y", "xh")
    both = P(store, tp)
    specs = (
        both, both, P(store, None, tp), P(store, None), P(store, None), P(store), P(store), P(tp, store),
        both, both, both, both, both, P(tp), P(tp), P(tp),
    )
    return jax.shard_map(shards, mesh=fine, in_specs=specs, out_specs=(both, both), check_vma=False)
```

```python
import functools

import jax
import jax.numpy as jnp
from jax import lax
from jax.experimental import pallas as pl
from jax.experimental.pallas import tpu as pltpu
from jax.sharding import Mesh, PartitionSpec as P

HD = 128
HEADS = 8
NS = 256
PAGE = 256
SP = 8
CAP = 2
PMAX = 28
HITS = 36
POOL = 32
ROWS = 128
NZ = 8
NTP = 8
VISITS = 32
MASKED = -1e30
SCALE = HD ** (-0.5) * 1.4426950408889634
F32 = jnp.float32
BF16 = jnp.bfloat16
VMEM_LIMIT = 60 * 1024 * 1024
PIECE = 256
TALL = HD + 16
LANES = 128
QUICK = pl.CostEstimate(flops=1024, bytes_accessed=1024, transcendentals=0)


def whole(shape):
    return pl.BlockSpec(shape, lambda *_: (0,) * len(shape))


def product(keys, q_ref, at):
    return [
        jnp.dot(keys, q_ref[at, :, pl.ds(lo, PIECE)], preferred_element_type=F32)
        for lo in range(0, HEADS * ROWS, PIECE)
    ]


def values(block):
    turned = block.astype(F32).T.astype(BF16)
    return jnp.concatenate([turned, jnp.ones((TALL - HD, block.shape[0]), BF16)], axis=0)


def absorb(pieces, values_t, at, shift, acc, top):
    for lo, raw in zip(range(0, HEADS * ROWS, PIECE), pieces):
        span = pl.ds(lo, PIECE)
        old = top[pl.ds(at, 1), span]
        new = jnp.maximum(old, jnp.max(raw, axis=0, keepdims=True) * SCALE + shift)
        expo = jnp.exp2(raw * SCALE - (new - shift))
        keep = jnp.exp2(old - new)
        top[pl.ds(at, 1), span] = new
        add = jnp.dot(values_t, expo.astype(BF16), preferred_element_type=F32)
        acc[at, :, span] = acc[at, :, span] * keep + add


def visit_kernel(first, tbl, meta, q_ref, *refs):
    if first:
        kv_ref, a_ref, b_ref, acc_out, top_out, acc, top, held, sems = refs
    else:
        acc_in, top_in, a_ref, b_ref, *outs, stats_ref, acc, top, held, sems, acc_was, acc_sem = refs
    width = HEADS * ROWS
    count = meta[0]
    turns = (count + 1) >> 1

    def fetch(turn):
        for side in range(2):
            item = tbl[turn * 2 + side]
            slot = (turn & 1) * 2 + side

            @pl.when(((item >> 5) & 1) == 1)
            def _():
                pltpu.make_async_copy(a_ref.at[item & 31], held.at[slot], sems.at[slot]).start()

            @pl.when(((item >> 5) & 1) == 0)
            def _():
                pltpu.make_async_copy(b_ref.at[item & 31], held.at[slot], sems.at[slot]).start()

    pl.when(turns > 0)(lambda: fetch(0))
    if not first:
        pltpu.make_async_copy(acc_in, acc_was, acc_sem).start()
    acc[...] = jnp.zeros_like(acc)
    top[...] = jnp.full_like(top, MASKED)
    if first:
        token = lax.broadcasted_iota(jnp.int32, (ROWS, PIECE), 0)
        row = lax.broadcasted_iota(jnp.int32, (ROWS, PIECE), 1) & (ROWS - 1)
        visible = (token <= row) & (token < meta[2])
        pieces = [jnp.where(visible, raw, MASKED) for raw in product(kv_ref[:, :HD], q_ref, meta[1])]
        absorb(pieces, values(kv_ref[:, HD:]), meta[1], 0.0, acc, top)

    def one(turn, carry):
        base = (turn & 1) * 2
        for side in range(2):
            pltpu.make_async_copy(a_ref.at[0], held.at[base + side], sems.at[base + side]).wait()
        pl.when(turn + 1 < turns)(lambda: fetch(turn + 1))
        places = [tbl[turn * 2 + side] >> 6 for side in range(2)]
        pieces = [product(held[base + side, :, :HD], q_ref, places[side]) for side in range(2)]
        values_t = [values(held[base + side, :, HD:]) for side in range(2)]
        absent = jnp.where(turn * 2 + 1 < count, 0.0, 2 * MASKED)
        absorb(pieces[0], values_t[0], places[0], 0.0, acc, top)
        absorb(pieces[1], values_t[1], places[1], absent, acc, top)
        return carry

    lax.fori_loop(0, turns, one, 0)

    if first:
        acc_out[...] = acc[...]
        top_out[...] = top[...]
    else:
        pltpu.make_async_copy(acc_in, acc_was, acc_sem).wait()
        for k, out in enumerate(outs):
            at = (meta[1] + k) & (NZ - 1)
            row = pl.ds(at, 1)
            now, was = top[row, :], top_in[row, :]
            both = jnp.maximum(now, was)
            keep, keep_was = jnp.exp2(now - both), jnp.exp2(was - both)
            total = acc[at, HD : HD + 1, :] * keep + acc_was[at, HD : HD + 1, :] * keep_was
            safe = jnp.where(total > 0, total, 1.0)
            keep, keep_was = keep / safe, keep_was / safe
            out[...] = (acc[at, 0:HD, :] * keep + acc_was[at, 0:HD, :] * keep_was).astype(BF16)
            weight = both + jnp.log2(safe)
            for head in range(HEADS):
                stats_ref[at, head : head + 1, :] = weight[:, head * ROWS : (head + 1) * ROWS]


def visit(first, tbl, meta, q_t, given, pages_a, pages_b):
    width = HEADS * ROWS
    state = [(NZ, TALL, width), (NZ, width)]
    anywhere = pl.BlockSpec(memory_space=pl.ANY)
    scratch = [pltpu.VMEM(s, F32) for s in state]
    scratch += [pltpu.VMEM((4, PAGE, 2 * HD), BF16), pltpu.SemaphoreType.DMA((4,))]
    if first:
        out_shape = [jax.ShapeDtypeStruct(s, F32) for s in state]
        given_specs = [whole(given[0].shape)]
    else:
        out_shape = [jax.ShapeDtypeStruct((HD, width), BF16)] * NZ
        out_shape.append(jax.ShapeDtypeStruct((NZ, HEADS, ROWS), F32))
        given_specs = [anywhere, whole(given[1].shape)]
        scratch += [pltpu.VMEM(state[0], F32), pltpu.SemaphoreType.DMA]
    return pl.pallas_call(
        functools.partial(visit_kernel, first),
        grid_spec=pltpu.PrefetchScalarGridSpec(
            num_scalar_prefetch=2,
            grid=(1,),
            in_specs=[whole(q_t.shape)] + given_specs + [anywhere] * 2,
            out_specs=[whole(o.shape) for o in out_shape],
            scratch_shapes=scratch,
        ),
        out_shape=out_shape,
        compiler_params=pltpu.CompilerParams(vmem_limit_bytes=VMEM_LIMIT),
        cost_estimate=QUICK,
    )(tbl, meta, q_t, *given, pages_a, pages_b)


def carry_kernel(n, tbl, pick, c_ref, *refs):
    pages, out = refs[: 4 * n], refs[4 * n]
    k = pl.program_id(0)
    for slot in range(4):
        page = pages[slot * n][0]
        if n == 2:
            page = jnp.where(pick[k * 4 + slot] == 0, page, pages[slot * n + 1][0])
        out[0, slot] = lax.dot_general(
            c_ref[0], page, (((1,), (1,)), ((), ())), preferred_element_type=F32
        ).astype(BF16)


def carry(tbl, pick, shift, c_rows, sources):
    n = len(sources[0])
    specs, given = [], []

    def where(slot, part, size):
        def index(k, tbl, pick):
            here = pick[k * 4 + slot] == part
            return (jnp.where(here, tbl[k * 4 + slot], 0), 0, 0)

        return pl.BlockSpec((1, PAGE, NS), index)

    for slot in range(4):
        for part in range(n):
            given.append(sources[slot // 2][part])
            specs.append(where(slot, part, given[-1].shape[0]))
    return pl.pallas_call(
        functools.partial(carry_kernel, n),
        grid_spec=pltpu.PrefetchScalarGridSpec(
            num_scalar_prefetch=2,
            grid=(NZ,),
            in_specs=[pl.BlockSpec((1, ROWS, NS), lambda k, tbl, pick: (k, 0, 0))] + specs,
            out_specs=pl.BlockSpec((1, 4, ROWS, PAGE), lambda k, tbl, pick: (k, 0, 0, 0)),
        ),
        out_shape=jax.ShapeDtypeStruct((NZ, 4, ROWS, PAGE), BF16),
        compiler_params=pltpu.CompilerParams(vmem_limit_bytes=VMEM_LIMIT),
        cost_estimate=QUICK,
    )(tbl, pick, c_rows, *given)


def join_kernel(scalars, stats_ref, *refs):
    parts, out = refs[:NZ], refs[NZ]
    weights = []
    for k in range(NZ):
        stats = stats_ref[(scalars[1] - k) & (NZ - 1)]
        weights.append(jnp.concatenate([stats[head : head + 1] for head in range(HEADS)], axis=1))
    top = functools.reduce(jnp.maximum, weights)
    weights = [jnp.exp2(w - top) for w in weights]
    row = lax.broadcasted_iota(jnp.int32, (1, HEADS * ROWS), 1) & (ROWS - 1)
    scale = jnp.where(row < scalars[0], 1.0 / functools.reduce(jnp.add, weights), 0.0)
    weights = [w * scale for w in weights]
    for head in range(HEADS):
        span = pl.ds(head * ROWS, ROWS)
        total = sum(
            p[:, span].astype(F32) * w[:, head * ROWS : (head + 1) * ROWS]
            for p, w in zip(parts, weights)
        )
        out[:, span] = total.T.astype(BF16)


def join(scalars, stats, parts):
    return pl.pallas_call(
        join_kernel,
        grid_spec=pltpu.PrefetchScalarGridSpec(
            num_scalar_prefetch=1,
            grid=(1,),
            in_specs=[whole(stats.shape)] + [whole(p.shape) for p in parts],
            out_specs=whole((ROWS, HEADS * HD)),
        ),
        out_shape=jax.ShapeDtypeStruct((ROWS, HEADS * HD), BF16),
        compiler_params=pltpu.CompilerParams(vmem_limit_bytes=VMEM_LIMIT),
        cost_estimate=QUICK,
    )(scalars, stats, *parts)


def inner_kernel(
    x_ref, z_ref, b_ref, c_ref, cum_ref, cum_t_ref, dt_t_ref, skip_ref, base_ref, grown_ref, gate_ref, products
):
    heads = cum_ref.shape[2]
    width = x_ref.shape[1]

    @pl.when(pl.program_id(0) == 0)
    def _():
        products[...] = lax.dot_general(
            c_ref[...], b_ref[...], (((1,), (1,)), ((), ())), preferred_element_type=F32
        )

    x = x_ref[...].astype(F32)
    causal = lax.broadcasted_iota(jnp.int32, (ROWS, ROWS), 0) >= lax.broadcasted_iota(jnp.int32, (ROWS, ROWS), 1)
    head_of = lax.broadcasted_iota(jnp.int32, (ROWS, width), 1) >> 6
    within = jnp.zeros((ROWS, width), F32)
    grown = jnp.zeros((ROWS, width), F32)
    for head in range(heads):
        column = cum_ref[0, :, head : head + 1]
        spread = jnp.where(causal, column - cum_t_ref[0, head : head + 1, :], MASKED)
        mixing = jnp.exp(spread) * products[...] * dt_t_ref[0, head : head + 1, :]
        mine = jnp.where(head_of == head, x, 0.0).astype(BF16)
        within += jnp.dot(mixing.astype(BF16), mine, preferred_element_type=F32)
        grown = jnp.where(head_of == head, jnp.exp(column), grown)
    gate = z_ref[...].astype(F32)
    base_ref[...] = within + skip_ref[...] * x
    grown_ref[...] = grown
    gate_ref[...] = gate / (1.0 + jnp.exp(-gate))


def inner(x, z, b, c, cum, dt, d_skip):
    heads = cum.shape[1] // SP
    width = x.shape[1] // SP
    cum4 = cum.reshape(ROWS, SP, heads).transpose(1, 0, 2)
    cum_t = cum.T.reshape(SP, heads, ROWS)
    dt_t = dt.T.reshape(SP, heads, ROWS)
    skip = jnp.repeat(d_skip, width // heads)[None]
    columns = pl.BlockSpec((ROWS, width), lambda i: (0, i))
    stack = lambda *s: pl.BlockSpec((1,) + s, lambda i: (i, 0, 0))
    return pl.pallas_call(
        inner_kernel,
        grid=(SP,),
        in_specs=[
            columns,
            columns,
            whole(b.shape),
            whole(c.shape),
            stack(ROWS, heads),
            stack(heads, ROWS),
            stack(heads, ROWS),
            pl.BlockSpec((1, width), lambda i: (0, i)),
        ],
        out_specs=[columns] * 3,
        scratch_shapes=[pltpu.VMEM((ROWS, ROWS), F32)],
        out_shape=[jax.ShapeDtypeStruct(x.shape, F32)] * 3,
        compiler_params=pltpu.CompilerParams(vmem_limit_bytes=VMEM_LIMIT),
        cost_estimate=QUICK,
    )(x, z, b, c, cum4, cum_t, dt_t, skip)


def finish_kernel(where, pick, length, base_ref, grown_ref, gate_ref, gain_ref, near_ref, far_ref, out_ref, gated, squares):
    step = pl.program_id(0)
    width = base_ref.shape[1]

    @pl.when(step == 0)
    def _():
        squares[...] = jnp.zeros_like(squares)

    got = jnp.where(pick[step] == 0, near_ref[0], far_ref[0]).astype(F32)
    value = (base_ref[...] + grown_ref[...] * got) * gate_ref[...]
    gated[step] = value
    squares[...] += value * value

    @pl.when(step == pl.num_programs(0) - 1)
    def _():
        mean = jnp.sum(squares[...], axis=1, keepdims=True) / (SP * PAGE)
        row = lax.broadcasted_iota(jnp.int32, (ROWS, 1), 0)
        scale = jnp.where(row < length[0], lax.rsqrt(mean + 1e-05), 0.0)
        for part in range(SP):
            span = slice(part * width, (part + 1) * width)
            out_ref[:, span] = (gated[part] * scale * gain_ref[:, span]).astype(BF16)


def finish(where, pick, length, base, grown, gate, gain, near, far):
    width = base.shape[1] // SP
    columns = pl.BlockSpec((ROWS, width), lambda i, w, p, n: (0, i))

    def block(chosen):
        return pl.BlockSpec((1, ROWS, width), lambda i, w, p, n: (jnp.where(p[i] == chosen, w[i], 0), 0, 0))

    return pl.pallas_call(
        finish_kernel,
        grid_spec=pltpu.PrefetchScalarGridSpec(
            num_scalar_prefetch=3,
            grid=(SP,),
            in_specs=[columns] * 3 + [whole((1, SP * width)), block(0), block(1)],
            out_specs=whole((ROWS, SP * width)),
            scratch_shapes=[pltpu.VMEM((SP, ROWS, width), F32), pltpu.VMEM((ROWS, width), F32)],
        ),
        out_shape=jax.ShapeDtypeStruct((ROWS, SP * width), BF16),
        compiler_params=pltpu.CompilerParams(vmem_limit_bytes=VMEM_LIMIT),
        cost_estimate=QUICK,
    )(where, pick, length, base, grown, gate, gain[None], near, far)


def listing(chosen, value):
    place = jnp.cumsum(chosen.astype(jnp.int32)) - 1
    slot = jnp.arange(VISITS)[:, None]
    hot = chosen[None, :] & (place[None, :] == slot)
    return jnp.sum(jnp.where(hot, value[None, :], 0), axis=1), jnp.sum(chosen.astype(jnp.int32))


def ranks(owners):
    order = jnp.arange(owners.shape[-1])
    earlier = order[None, :] < order[:, None]
    same = owners[..., :, None] == owners[..., None, :]
    return jnp.sum((same & earlier).astype(jnp.int32), axis=-1)


def tie(*trees):
    return lax.optimization_barrier(trees)


def shards(
    queries, kv_new, page_pool, hit_owner, hit_page, prefix_blocks, suffix_len, out_weight,
    mamba_x, mamba_z, mamba_b, mamba_c, mamba_dt, a_log, d_skip, norm_gain,
):
    me_x, me_z, me_c = lax.axis_index("xl"), lax.axis_index("z"), lax.axis_index("co")
    me_t = lax.axis_index(("y", "xh"))
    swap = [(0, 1), (1, 0)]

    far = lax.ppermute(page_pool, "xl", swap)
    own_b = lax.ppermute(page_pool, "co", swap)
    numbers = jnp.concatenate([hit_owner[0], hit_page[0], prefix_blocks]).astype(BF16)
    packed = jnp.concatenate([mamba_c, jnp.pad(numbers[None, :], ((0, 15), (0, NS - numbers.shape[0])))], axis=0)
    shared = lax.all_to_all(jnp.broadcast_to(packed[None], (NZ,) + packed.shape), "z", 0, 0, tiled=True)
    q_t = queries.reshape(ROWS, HEADS, HD).transpose(2, 1, 0).reshape(HD, HEADS * ROWS)
    q_all = lax.all_gather(q_t, "z", axis=0, tiled=False)

    table = shared[:, ROWS, : 2 * HITS + 1].astype(jnp.int32)
    owners, page_ids, live = table[:, :HITS], table[:, HITS : 2 * HITS], table[:, 2 * HITS]
    mine = (owners // 2) % NZ == me_z
    near = owners // 16 == me_x
    same_core = owners % 2 == me_c
    request = jnp.broadcast_to(jnp.arange(NZ)[:, None], owners.shape)
    wanted = mine & (jnp.arange(HITS)[None, :] < jnp.minimum(live, PMAX)[:, None])

    def listed(chosen, ids):
        value = ids + 32 * same_core.astype(jnp.int32) + 64 * request
        flat = lambda a: a[:, :PMAX].reshape(-1)
        tbl, count = listing(flat(wanted & chosen), flat(value))
        return tbl, jnp.stack([count, me_z, suffix_len[0]])

    tbl_near, meta_near = listed(near, page_ids)
    tbl_far, meta_far = listed(~near, page_ids)

    held, held_ids = owners[:, PMAX:], page_ids[:, PMAX:]
    held_slot = 2 * (held % 2 != me_c).astype(jnp.int32) + ranks(held)

    def slots(chosen):
        hot = chosen[:, None, :] & (held_slot[:, None, :] == jnp.arange(4)[None, :, None])
        return jnp.sum(jnp.where(hot, held_ids[:, None, :], 0), axis=2).reshape(-1)

    c_rows = shared[:, :ROWS]
    held_here = mine[:, PMAX:]
    held_near = near[:, PMAX:]
    ids_near = slots(held_here & held_near)
    ids_far = slots(held_here & ~held_near)
    none = jnp.zeros_like(ids_near)
    sent_near = carry(ids_near, none, me_z, c_rows, [[page_pool], [own_b]])
    got_near = lax.all_to_all(sent_near, "z", 0, 0, tiled=True)

    cum = jnp.cumsum(-jnp.exp(a_log)[None, :] * mamba_dt, axis=0)
    base, grown, gate = inner(mamba_x, mamba_z, mamba_b, mamba_c, cum, mamba_dt, d_skip)
    q_all, base = tie(q_all, base)
    state = visit(True, tbl_near, meta_near, q_all, [kv_new], page_pool, own_b)
    far, got_near, state = tie(far, got_near, state)
    far_b = lax.ppermute(far, "co", swap)
    *parts, stats = visit(False, tbl_far, meta_far, q_all, state, far, far_b)
    out_weight, far = tie(out_weight, far)
    pieces = []
    upper = me_z // 4
    for k in range(2):
        piece = jnp.where(upper == k, out_weight[:, :LANES], out_weight[:, LANES:])
        pairs = []
        for z in range(NZ):
            for core in range(2):
                goal = 4 * (z % 2) + 2 * core + ((z // 4) ^ k)
                pairs.append((z * 2 + core, goal * 2 + (z // 2) % 2))
        pieces.append(lax.ppermute(piece, ("z", "co"), pairs))
    c_rows, pieces, parts = tie(c_rows, pieces, parts)
    parts = [
        a if k == 0 else lax.ppermute(a, "z", [(i, (i + k) % NZ) for i in range(NZ)])
        for k, a in enumerate(parts)
    ]
    sent_far = carry(ids_far, none, me_z, c_rows, [[far], [far_b]])

    parts[1], stats = tie(parts[1], stats)
    stats = lax.all_to_all(stats, "z", 0, 0, tiled=True)
    parts, stats, sent_far = tie(parts, stats, sent_far)
    attn_out = join(jnp.stack([suffix_len[0], me_z]), stats, parts)
    odd = me_z % 2 == 1
    halves = jnp.stack([jnp.where(odd, pieces[1], pieces[0]), jnp.where(odd, pieces[0], pieces[1])])
    weight = lax.all_gather(halves, ("xl", "co"), axis=0, tiled=True)
    attn_out, weight = tie(attn_out, weight)
    up = [(i, (i + 1) % NZ) for i in range(NZ)]
    down = [(i, (i - 1) % NZ) for i in range(NZ)]
    ahead, behind = [attn_out], [attn_out]
    for _ in range(NZ // 2 - 1):
        ahead.append(lax.ppermute(ahead[-1], "z", up))
        behind.append(lax.ppermute(behind[-1], "z", down))
    middle = ROWS // 2
    across = [lax.ppermute(ahead[-1][:middle], "z", up), lax.ppermute(behind[-1][middle:], "z", down)]
    gathered = jnp.concatenate(behind + across + ahead[:0:-1], axis=0)
    gathered, sent_far = tie(gathered, sent_far)
    got_far = lax.all_to_all(sent_far, "z", 0, 0, tiled=True)
    def product_for(t):
        block = lax.dynamic_index_in_dim(weight, (t // 4) * 4 + (t % 2) * 2 + (t // 2) % 2, 0, keepdims=False)
        return jnp.dot(gathered, block, preferred_element_type=F32)

    total = product_for(me_t)
    for k in range(1, NTP):
        sent = product_for(me_t ^ k).astype(BF16)
        total += lax.ppermute(sent, ("y", "xh"), [(i, i ^ k) for i in range(NTP)]).astype(F32)
    total = total.astype(BF16).reshape(NZ, ROWS, LANES)
    total = lax.dynamic_slice_in_dim(jnp.concatenate([total, total], axis=0), (NZ - me_z) % NZ, NZ, axis=0)
    total, got_far = tie(total, got_far)
    columns = lax.all_to_all(total, "z", 0, 0, tiled=True)
    attn_proj = columns.transpose(1, 0, 2).reshape(ROWS, NZ * LANES)

    from_owner = hit_owner[0, PMAX:]
    slot = 2 * (from_owner % 2 != me_c).astype(jnp.int32) + ranks(from_owner)
    where = (from_owner // 2) % NZ * 4 + slot
    pick = (from_owner // 16 != me_x).astype(jnp.int32)
    flat = lambda a: a.reshape(4 * NZ, ROWS, PAGE)
    mamba_out = finish(where, pick, suffix_len, base, grown, gate, norm_gain, flat(got_near), flat(got_far))
    return (attn_proj, mamba_out)


def solution(mesh):
    fine = Mesh(mesh.devices.reshape(2, 8, 2, 4, 2), ("xl", "z", "co", "y", "xh"))
    store, tp = ("xl", "z", "co"), ("y", "xh")
    both = P(store, tp)
    specs = (
        both, both, P(store, None, tp), P(store, None), P(store, None), P(store), P(store), P(tp, store),
        both, both, both, both, both, P(tp), P(tp), P(tp),
    )
    return jax.shard_map(shards, mesh=fine, in_specs=specs, out_specs=(both, both), check_vma=False)
```

```python
import functools

import jax
import jax.numpy as jnp
from jax import lax
from jax.experimental import pallas as pl
from jax.experimental.pallas import tpu as pltpu
from jax.sharding import Mesh, PartitionSpec as P

HD = 128
HEADS = 8
NS = 256
PAGE = 256
SP = 8
CAP = 2
PMAX = 28
HITS = 36
POOL = 32
ROWS = 128
NZ = 8
NTP = 8
VISITS = 32
MASKED = -1e30
SCALE = HD ** (-0.5) * 1.4426950408889634
F32 = jnp.float32
BF16 = jnp.bfloat16
VMEM_LIMIT = 60 * 1024 * 1024
PIECE = 256
TALL = HD + 16
LANES = 128
QUICK = pl.CostEstimate(flops=1024, bytes_accessed=1024, transcendentals=0)


def whole(shape):
    return pl.BlockSpec(shape, lambda *_: (0,) * len(shape))


def product(keys, q_ref, at):
    return [
        jnp.dot(keys, q_ref[at, :, pl.ds(lo, PIECE)], preferred_element_type=F32)
        for lo in range(0, HEADS * ROWS, PIECE)
    ]


def values(block):
    turned = block.astype(F32).T.astype(BF16)
    return jnp.concatenate([turned, jnp.ones((TALL - HD, block.shape[0]), BF16)], axis=0)


def absorb_one(lo, raw, values_t, at, shift, acc, top):
    span = pl.ds(lo, PIECE)
    old = top[pl.ds(at, 1), span]
    new = jnp.maximum(old, jnp.max(raw, axis=0, keepdims=True) * SCALE + shift)
    expo = jnp.exp2(raw * SCALE - (new - shift))
    keep = jnp.exp2(old - new)
    top[pl.ds(at, 1), span] = new
    add = jnp.dot(values_t, expo.astype(BF16), preferred_element_type=F32)
    acc[at, :, span] = acc[at, :, span] * keep + add


def absorb(pieces, values_t, at, shift, acc, top):
    for lo, raw in zip(range(0, HEADS * ROWS, PIECE), pieces):
        absorb_one(lo, raw, values_t, at, shift, acc, top)


def visit_kernel(first, tbl, meta, q_ref, *refs):
    if first:
        kv_ref, a_ref, b_ref, acc_out, top_out, acc, top, held, sems = refs
    else:
        acc_in, top_in, a_ref, b_ref, *outs, stats_ref, acc, top, held, sems, acc_was, acc_sem = refs
    width = HEADS * ROWS
    count = meta[0]
    turns = (count + 1) >> 1

    def fetch(turn):
        for side in range(2):
            item = tbl[turn * 2 + side]
            slot = (turn & 1) * 2 + side

            @pl.when(((item >> 5) & 1) == 1)
            def _():
                pltpu.make_async_copy(a_ref.at[item & 31], held.at[slot], sems.at[slot]).start()

            @pl.when(((item >> 5) & 1) == 0)
            def _():
                pltpu.make_async_copy(b_ref.at[item & 31], held.at[slot], sems.at[slot]).start()

    pl.when(turns > 0)(lambda: fetch(0))
    if not first:
        pltpu.make_async_copy(acc_in, acc_was, acc_sem).start()
    acc[...] = jnp.zeros_like(acc)
    top[...] = jnp.full_like(top, MASKED)
    if first:
        token = lax.broadcasted_iota(jnp.int32, (ROWS, PIECE), 0)
        row = lax.broadcasted_iota(jnp.int32, (ROWS, PIECE), 1) & (ROWS - 1)
        visible = (token <= row) & (token < meta[2])
        pieces = [jnp.where(visible, raw, MASKED) for raw in product(kv_ref[:, :HD], q_ref, meta[1])]
        absorb(pieces, values(kv_ref[:, HD:]), meta[1], 0.0, acc, top)

    def one(turn, carry):
        base = (turn & 1) * 2
        for side in range(2):
            pltpu.make_async_copy(a_ref.at[0], held.at[base + side], sems.at[base + side]).wait()
        pl.when(turn + 1 < turns)(lambda: fetch(turn + 1))
        places = [tbl[turn * 2 + side] >> 6 for side in range(2)]
        pieces = [product(held[base + side, :, :HD], q_ref, places[side]) for side in range(2)]
        values_t = [values(held[base + side, :, HD:]) for side in range(2)]
        absent = jnp.where(turn * 2 + 1 < count, 0.0, 2 * MASKED)
        for part, lo in enumerate(range(0, HEADS * ROWS, PIECE)):
            absorb_one(lo, pieces[0][part], values_t[0], places[0], 0.0, acc, top)
            absorb_one(lo, pieces[1][part], values_t[1], places[1], absent, acc, top)
        return carry

    lax.fori_loop(0, turns, one, 0)

    if first:
        acc_out[...] = acc[...]
        top_out[...] = top[...]
    else:
        pltpu.make_async_copy(acc_in, acc_was, acc_sem).wait()
        for k, out in enumerate(outs):
            at = (meta[1] + k) & (NZ - 1)
            row = pl.ds(at, 1)
            now, was = top[row, :], top_in[row, :]
            both = jnp.maximum(now, was)
            keep, keep_was = jnp.exp2(now - both), jnp.exp2(was - both)
            total = acc[at, HD : HD + 1, :] * keep + acc_was[at, HD : HD + 1, :] * keep_was
            safe = jnp.where(total > 0, total, 1.0)
            keep, keep_was = keep / safe, keep_was / safe
            out[...] = (acc[at, 0:HD, :] * keep + acc_was[at, 0:HD, :] * keep_was).astype(BF16)
            weight = both + jnp.log2(safe)
            for head in range(HEADS):
                stats_ref[at, head : head + 1, :] = weight[:, head * ROWS : (head + 1) * ROWS]


def visit(first, tbl, meta, q_t, given, pages_a, pages_b):
    width = HEADS * ROWS
    state = [(NZ, TALL, width), (NZ, width)]
    anywhere = pl.BlockSpec(memory_space=pl.ANY)
    scratch = [pltpu.VMEM(s, F32) for s in state]
    scratch += [pltpu.VMEM((4, PAGE, 2 * HD), BF16), pltpu.SemaphoreType.DMA((4,))]
    if first:
        out_shape = [jax.ShapeDtypeStruct(s, F32) for s in state]
        given_specs = [whole(given[0].shape)]
    else:
        out_shape = [jax.ShapeDtypeStruct((HD, width), BF16)] * NZ
        out_shape.append(jax.ShapeDtypeStruct((NZ, HEADS, ROWS), F32))
        given_specs = [anywhere, whole(given[1].shape)]
        scratch += [pltpu.VMEM(state[0], F32), pltpu.SemaphoreType.DMA]
    return pl.pallas_call(
        functools.partial(visit_kernel, first),
        grid_spec=pltpu.PrefetchScalarGridSpec(
            num_scalar_prefetch=2,
            grid=(1,),
            in_specs=[whole(q_t.shape)] + given_specs + [anywhere] * 2,
            out_specs=[whole(o.shape) for o in out_shape],
            scratch_shapes=scratch,
        ),
        out_shape=out_shape,
        compiler_params=pltpu.CompilerParams(vmem_limit_bytes=VMEM_LIMIT),
        cost_estimate=QUICK,
    )(tbl, meta, q_t, *given, pages_a, pages_b)


def carry_kernel(n, tbl, pick, c_ref, *refs):
    pages, out = refs[: 4 * n], refs[4 * n]
    k = pl.program_id(0)
    for slot in range(4):
        page = pages[slot * n][0]
        if n == 2:
            page = jnp.where(pick[k * 4 + slot] == 0, page, pages[slot * n + 1][0])
        out[0, slot] = lax.dot_general(
            c_ref[0], page, (((1,), (1,)), ((), ())), preferred_element_type=F32
        ).astype(BF16)


def carry(tbl, pick, shift, c_rows, sources):
    n = len(sources[0])
    specs, given = [], []

    def where(slot, part, size):
        def index(k, tbl, pick):
            here = pick[k * 4 + slot] == part
            return (jnp.where(here, tbl[k * 4 + slot], 0), 0, 0)

        return pl.BlockSpec((1, PAGE, NS), index)

    for slot in range(4):
        for part in range(n):
            given.append(sources[slot // 2][part])
            specs.append(where(slot, part, given[-1].shape[0]))
    return pl.pallas_call(
        functools.partial(carry_kernel, n),
        grid_spec=pltpu.PrefetchScalarGridSpec(
            num_scalar_prefetch=2,
            grid=(NZ,),
            in_specs=[pl.BlockSpec((1, ROWS, NS), lambda k, tbl, pick: (k, 0, 0))] + specs,
            out_specs=pl.BlockSpec((1, 4, ROWS, PAGE), lambda k, tbl, pick: (k, 0, 0, 0)),
        ),
        out_shape=jax.ShapeDtypeStruct((NZ, 4, ROWS, PAGE), BF16),
        compiler_params=pltpu.CompilerParams(vmem_limit_bytes=VMEM_LIMIT),
        cost_estimate=QUICK,
    )(tbl, pick, c_rows, *given)


def join_kernel(scalars, stats_ref, *refs):
    parts, out = refs[:NZ], refs[NZ]
    weights = []
    for k in range(NZ):
        stats = stats_ref[(scalars[1] - k) & (NZ - 1)]
        weights.append(jnp.concatenate([stats[head : head + 1] for head in range(HEADS)], axis=1))
    top = functools.reduce(jnp.maximum, weights)
    weights = [jnp.exp2(w - top) for w in weights]
    row = lax.broadcasted_iota(jnp.int32, (1, HEADS * ROWS), 1) & (ROWS - 1)
    scale = jnp.where(row < scalars[0], 1.0 / functools.reduce(jnp.add, weights), 0.0)
    weights = [w * scale for w in weights]
    for head in range(HEADS):
        span = pl.ds(head * ROWS, ROWS)
        total = sum(
            p[:, span].astype(F32) * w[:, head * ROWS : (head + 1) * ROWS]
            for p, w in zip(parts, weights)
        )
        out[:, span] = total.T.astype(BF16)


def join(scalars, stats, parts):
    return pl.pallas_call(
        join_kernel,
        grid_spec=pltpu.PrefetchScalarGridSpec(
            num_scalar_prefetch=1,
            grid=(1,),
            in_specs=[whole(stats.shape)] + [whole(p.shape) for p in parts],
            out_specs=whole((ROWS, HEADS * HD)),
        ),
        out_shape=jax.ShapeDtypeStruct((ROWS, HEADS * HD), BF16),
        compiler_params=pltpu.CompilerParams(vmem_limit_bytes=VMEM_LIMIT),
        cost_estimate=QUICK,
    )(scalars, stats, *parts)


def inner_kernel(
    x_ref, z_ref, b_ref, c_ref, cum_ref, cum_t_ref, dt_t_ref, skip_ref, base_ref, grown_ref, gate_ref, products
):
    heads = cum_ref.shape[2]
    width = x_ref.shape[1]

    @pl.when(pl.program_id(0) == 0)
    def _():
        products[...] = lax.dot_general(
            c_ref[...], b_ref[...], (((1,), (1,)), ((), ())), preferred_element_type=F32
        )

    x = x_ref[...].astype(F32)
    causal = lax.broadcasted_iota(jnp.int32, (ROWS, ROWS), 0) >= lax.broadcasted_iota(jnp.int32, (ROWS, ROWS), 1)
    head_of = lax.broadcasted_iota(jnp.int32, (ROWS, width), 1) >> 6
    within = jnp.zeros((ROWS, width), F32)
    grown = jnp.zeros((ROWS, width), F32)
    for head in range(heads):
        column = cum_ref[0, :, head : head + 1]
        spread = jnp.where(causal, column - cum_t_ref[0, head : head + 1, :], MASKED)
        mixing = jnp.exp(spread) * products[...] * dt_t_ref[0, head : head + 1, :]
        mine = jnp.where(head_of == head, x, 0.0).astype(BF16)
        within += jnp.dot(mixing.astype(BF16), mine, preferred_element_type=F32)
        grown = jnp.where(head_of == head, jnp.exp(column), grown)
    gate = z_ref[...].astype(F32)
    base_ref[...] = within + skip_ref[...] * x
    grown_ref[...] = grown
    gate_ref[...] = gate / (1.0 + jnp.exp(-gate))


def inner(x, z, b, c, cum, dt, d_skip):
    heads = cum.shape[1] // SP
    width = x.shape[1] // SP
    cum4 = cum.reshape(ROWS, SP, heads).transpose(1, 0, 2)
    cum_t = cum.T.reshape(SP, heads, ROWS)
    dt_t = dt.T.reshape(SP, heads, ROWS)
    skip = jnp.repeat(d_skip, width // heads)[None]
    columns = pl.BlockSpec((ROWS, width), lambda i: (0, i))
    stack = lambda *s: pl.BlockSpec((1,) + s, lambda i: (i, 0, 0))
    return pl.pallas_call(
        inner_kernel,
        grid=(SP,),
        in_specs=[
            columns,
            columns,
            whole(b.shape),
            whole(c.shape),
            stack(ROWS, heads),
            stack(heads, ROWS),
            stack(heads, ROWS),
            pl.BlockSpec((1, width), lambda i: (0, i)),
        ],
        out_specs=[columns] * 3,
        scratch_shapes=[pltpu.VMEM((ROWS, ROWS), F32)],
        out_shape=[jax.ShapeDtypeStruct(x.shape, F32)] * 3,
        compiler_params=pltpu.CompilerParams(vmem_limit_bytes=VMEM_LIMIT),
        cost_estimate=QUICK,
    )(x, z, b, c, cum4, cum_t, dt_t, skip)


def finish_kernel(where, pick, length, base_ref, grown_ref, gate_ref, gain_ref, near_ref, far_ref, out_ref, gated, squares):
    step = pl.program_id(0)
    width = base_ref.shape[1]

    @pl.when(step == 0)
    def _():
        squares[...] = jnp.zeros_like(squares)

    got = jnp.where(pick[step] == 0, near_ref[0], far_ref[0]).astype(F32)
    value = (base_ref[...] + grown_ref[...] * got) * gate_ref[...]
    gated[step] = value
    squares[...] += value * value

    @pl.when(step == pl.num_programs(0) - 1)
    def _():
        mean = jnp.sum(squares[...], axis=1, keepdims=True) / (SP * PAGE)
        row = lax.broadcasted_iota(jnp.int32, (ROWS, 1), 0)
        scale = jnp.where(row < length[0], lax.rsqrt(mean + 1e-05), 0.0)
        for part in range(SP):
            span = slice(part * width, (part + 1) * width)
            out_ref[:, span] = (gated[part] * scale * gain_ref[:, span]).astype(BF16)


def finish(where, pick, length, base, grown, gate, gain, near, far):
    width = base.shape[1] // SP
    columns = pl.BlockSpec((ROWS, width), lambda i, w, p, n: (0, i))

    def block(chosen):
        return pl.BlockSpec((1, ROWS, width), lambda i, w, p, n: (jnp.where(p[i] == chosen, w[i], 0), 0, 0))

    return pl.pallas_call(
        finish_kernel,
        grid_spec=pltpu.PrefetchScalarGridSpec(
            num_scalar_prefetch=3,
            grid=(SP,),
            in_specs=[columns] * 3 + [whole((1, SP * width)), block(0), block(1)],
            out_specs=whole((ROWS, SP * width)),
            scratch_shapes=[pltpu.VMEM((SP, ROWS, width), F32), pltpu.VMEM((ROWS, width), F32)],
        ),
        out_shape=jax.ShapeDtypeStruct((ROWS, SP * width), BF16),
        compiler_params=pltpu.CompilerParams(vmem_limit_bytes=VMEM_LIMIT),
        cost_estimate=QUICK,
    )(where, pick, length, base, grown, gate, gain[None], near, far)


def listing(chosen, value):
    place = jnp.cumsum(chosen.astype(jnp.int32)) - 1
    slot = jnp.arange(VISITS)[:, None]
    hot = chosen[None, :] & (place[None, :] == slot)
    return jnp.sum(jnp.where(hot, value[None, :], 0), axis=1), jnp.sum(chosen.astype(jnp.int32))


def ranks(owners):
    order = jnp.arange(owners.shape[-1])
    earlier = order[None, :] < order[:, None]
    same = owners[..., :, None] == owners[..., None, :]
    return jnp.sum((same & earlier).astype(jnp.int32), axis=-1)


def tie(*trees):
    return lax.optimization_barrier(trees)


def shards(
    queries, kv_new, page_pool, hit_owner, hit_page, prefix_blocks, suffix_len, out_weight,
    mamba_x, mamba_z, mamba_b, mamba_c, mamba_dt, a_log, d_skip, norm_gain,
):
    me_x, me_z, me_c = lax.axis_index("xl"), lax.axis_index("z"), lax.axis_index("co")
    me_t = lax.axis_index(("y", "xh"))
    swap = [(0, 1), (1, 0)]

    far = lax.ppermute(page_pool, "xl", swap)
    own_b = lax.ppermute(page_pool, "co", swap)
    numbers = jnp.concatenate([hit_owner[0], hit_page[0], prefix_blocks]).astype(BF16)
    packed = jnp.concatenate([mamba_c, jnp.pad(numbers[None, :], ((0, 15), (0, NS - numbers.shape[0])))], axis=0)
    shared = lax.all_to_all(jnp.broadcast_to(packed[None], (NZ,) + packed.shape), "z", 0, 0, tiled=True)
    q_t = queries.reshape(ROWS, HEADS, HD).transpose(2, 1, 0).reshape(HD, HEADS * ROWS)
    q_all = lax.all_gather(q_t, "z", axis=0, tiled=False)

    table = shared[:, ROWS, : 2 * HITS + 1].astype(jnp.int32)
    owners, page_ids, live = table[:, :HITS], table[:, HITS : 2 * HITS], table[:, 2 * HITS]
    mine = (owners // 2) % NZ == me_z
    near = owners // 16 == me_x
    same_core = owners % 2 == me_c
    request = jnp.broadcast_to(jnp.arange(NZ)[:, None], owners.shape)
    wanted = mine & (jnp.arange(HITS)[None, :] < jnp.minimum(live, PMAX)[:, None])

    def listed(chosen, ids):
        value = ids + 32 * same_core.astype(jnp.int32) + 64 * request
        flat = lambda a: a[:, :PMAX].reshape(-1)
        tbl, count = listing(flat(wanted & chosen), flat(value))
        return tbl, jnp.stack([count, me_z, suffix_len[0]])

    tbl_near, meta_near = listed(near, page_ids)
    tbl_far, meta_far = listed(~near, page_ids)

    held, held_ids = owners[:, PMAX:], page_ids[:, PMAX:]
    held_slot = 2 * (held % 2 != me_c).astype(jnp.int32) + ranks(held)

    def slots(chosen):
        hot = chosen[:, None, :] & (held_slot[:, None, :] == jnp.arange(4)[None, :, None])
        return jnp.sum(jnp.where(hot, held_ids[:, None, :], 0), axis=2).reshape(-1)

    c_rows = shared[:, :ROWS]
    held_here = mine[:, PMAX:]
    held_near = near[:, PMAX:]
    ids_near = slots(held_here & held_near)
    ids_far = slots(held_here & ~held_near)
    none = jnp.zeros_like(ids_near)
    sent_near = carry(ids_near, none, me_z, c_rows, [[page_pool], [own_b]])
    got_near = lax.all_to_all(sent_near, "z", 0, 0, tiled=True)

    cum = jnp.cumsum(-jnp.exp(a_log)[None, :] * mamba_dt, axis=0)
    base, grown, gate = inner(mamba_x, mamba_z, mamba_b, mamba_c, cum, mamba_dt, d_skip)
    q_all, base = tie(q_all, base)
    state = visit(True, tbl_near, meta_near, q_all, [kv_new], page_pool, own_b)
    far, got_near, state = tie(far, got_near, state)
    far_b = lax.ppermute(far, "co", swap)
    *parts, stats = visit(False, tbl_far, meta_far, q_all, state, far, far_b)
    out_weight, far = tie(out_weight, far)
    pieces = []
    upper = me_z // 4
    for k in range(2):
        piece = jnp.where(upper == k, out_weight[:, :LANES], out_weight[:, LANES:])
        pairs = []
        for z in range(NZ):
            for core in range(2):
                goal = 4 * (z % 2) + 2 * core + ((z // 4) ^ k)
                pairs.append((z * 2 + core, goal * 2 + (z // 2) % 2))
        pieces.append(lax.ppermute(piece, ("z", "co"), pairs))
    c_rows, pieces, parts = tie(c_rows, pieces, parts)
    parts = [
        a if k == 0 else lax.ppermute(a, "z", [(i, (i + k) % NZ) for i in range(NZ)])
        for k, a in enumerate(parts)
    ]
    sent_far = carry(ids_far, none, me_z, c_rows, [[far], [far_b]])

    parts[1], stats = tie(parts[1], stats)
    stats = lax.all_to_all(stats, "z", 0, 0, tiled=True)
    parts, stats, sent_far = tie(parts, stats, sent_far)
    attn_out = join(jnp.stack([suffix_len[0], me_z]), stats, parts)
    odd = me_z % 2 == 1
    halves = jnp.stack([jnp.where(odd, pieces[1], pieces[0]), jnp.where(odd, pieces[0], pieces[1])])
    weight = lax.all_gather(halves, ("xl", "co"), axis=0, tiled=True)
    attn_out, weight = tie(attn_out, weight)
    up = [(i, (i + 1) % NZ) for i in range(NZ)]
    down = [(i, (i - 1) % NZ) for i in range(NZ)]
    ahead, behind = [attn_out], [attn_out]
    for _ in range(NZ // 2 - 1):
        ahead.append(lax.ppermute(ahead[-1], "z", up))
        behind.append(lax.ppermute(behind[-1], "z", down))
    middle = ROWS // 2
    across = [lax.ppermute(ahead[-1][:middle], "z", up), lax.ppermute(behind[-1][middle:], "z", down)]
    gathered = jnp.concatenate(behind + across + ahead[:0:-1], axis=0)
    gathered, sent_far = tie(gathered, sent_far)
    got_far = lax.all_to_all(sent_far, "z", 0, 0, tiled=True)
    def product_for(t):
        block = lax.dynamic_index_in_dim(weight, (t // 4) * 4 + (t % 2) * 2 + (t // 2) % 2, 0, keepdims=False)
        return jnp.dot(gathered, block, preferred_element_type=F32)

    total = product_for(me_t)
    for k in range(1, NTP):
        sent = product_for(me_t ^ k).astype(BF16)
        total += lax.ppermute(sent, ("y", "xh"), [(i, i ^ k) for i in range(NTP)]).astype(F32)
    total = total.astype(BF16).reshape(NZ, ROWS, LANES)
    total = lax.dynamic_slice_in_dim(jnp.concatenate([total, total], axis=0), (NZ - me_z) % NZ, NZ, axis=0)
    total, got_far = tie(total, got_far)
    columns = lax.all_to_all(total, "z", 0, 0, tiled=True)
    attn_proj = columns.transpose(1, 0, 2).reshape(ROWS, NZ * LANES)

    from_owner = hit_owner[0, PMAX:]
    slot = 2 * (from_owner % 2 != me_c).astype(jnp.int32) + ranks(from_owner)
    where = (from_owner // 2) % NZ * 4 + slot
    pick = (from_owner // 16 != me_x).astype(jnp.int32)
    flat = lambda a: a.reshape(4 * NZ, ROWS, PAGE)
    mamba_out = finish(where, pick, suffix_len, base, grown, gate, norm_gain, flat(got_near), flat(got_far))
    return (attn_proj, mamba_out)


def solution(mesh):
    fine = Mesh(mesh.devices.reshape(2, 8, 2, 4, 2), ("xl", "z", "co", "y", "xh"))
    store, tp = ("xl", "z", "co"), ("y", "xh")
    both = P(store, tp)
    specs = (
        both, both, P(store, None, tp), P(store, None), P(store, None), P(store), P(store), P(tp, store),
        both, both, both, both, both, P(tp), P(tp), P(tp),
    )
    return jax.shard_map(shards, mesh=fine, in_specs=specs, out_specs=(both, both), check_vma=False)
```
